512 devices in a mesh: gx: 4 (over x), gy: 4 (over y_lo), gz: 32 (over y_hi, z, core).
Axes of the slice: x: 4, y: 8 (y_hi: 2, y_lo: 4; y = y_hi * 4 + y_lo), z: 8, core: 2. Of those that a mesh axis runs over, the one named last changes fastest.
Arguments:
- features: bfloat16 [4, 4, 32, 256, 128], P('gx', 'gy', 'gz'), may hold values from -6 to 6
- positions: float32 [4, 4, 32, 3, 256], P('gx', 'gy', 'gz'), may hold values from 0 to 1
- counts: int32 [4, 4, 32], P('gx', 'gy', 'gz'), may hold values from 128 to 256, as said below
- pair_tiles: int32 [4, 4, 32, 14, 2, 2], P('gx', 'gy', 'gz'), may hold values from 0 to 7, as said below
- input_weight: bfloat16 [128, 128], replicated, may hold values from -0.5 to 0.5
- radial_weight: bfloat16 [128, 128], replicated, may hold values from -1.5 to 1.5
- radial_bias: float32 [128], replicated, may hold values from -3 to 3
- filter_weight: bfloat16 [128, 128], replicated, may hold values from -0.5 to 0.5
- filter_bias: float32 [128], replicated, may hold values from -3 to 3
- output_weight: bfloat16 [128, 128], replicated, may hold values from -0.1875 to 0.1875
- output_bias: float32 [128], replicated, may hold values from -3 to 3
- final_weight: bfloat16 [128, 128], replicated, may hold values from -0.5 to 0.5
- final_bias: float32 [128], replicated, may hold values from -3 to 3
- cotangent: bfloat16 [4, 4, 32, 256, 128], P('gx', 'gy', 'gz'), may hold values from -1.5 to 1.5
Outputs:
- new_features: bfloat16 [4, 4, 32, 256, 128], P('gx', 'gy', 'gz')
- grad_features: float32 [4, 4, 32, 256, 128], P('gx', 'gy', 'gz')
- forces: float32 [4, 4, 32, 3, 256], P('gx', 'gy', 'gz')
The draws below stay inside these ranges and needn't reach their ends.
Inputs may be any that keep to these rules, and one draw needn't show every extreme that they name: Block p holds counts[p] atoms in its first slots; the other slots are empty. Some block is full. `pair_tiles`: for each block and each of the 14 offsets, the 2 entries are distinct pairs (a, b) of tile numbers below 8; for offset 0 every pair has a <= b.
All inputs are finite; a program needn't handle non-finite values.
Results may differ from the reference program's by a relative error of at most 0.0085.
Values sent between devices are 32-bit elements; how exact they have to be, the bound alone decides.
No kernel may reach another device: no remote copies, remote signals or barrier semaphores. Data moves between devices by JAX's collectives and lax.ppermute only.
A program may use at most 192 MiB of HBM per device.

```python
import math
import jax
import jax.numpy as jnp
from jax import lax

A = 256
F = 128
K = 128
TILE = 32
TP = 2
BX = 4
BY = 4
BZ = 32


def draw_counts(key, part):
    key = jax.random.fold_in(key, 5)
    block_count = BX * BY * BZ
    drawn = A - jax.random.randint(key, (block_count,), 0, A // 2 + 1)
    chosen = jax.random.randint(jax.random.fold_in(key, 1), (), 0, block_count)
    filled = jnp.where(jnp.arange(block_count) == chosen, A, drawn)
    return filled.reshape(BX, BY, BZ).astype(jnp.int32)


def draw_pair_tiles(key, part):
    key = jax.random.fold_in(key, 11)
    tile_count = A // TILE
    cell_count = tile_count * tile_count
    block_count = BX * BY * BZ
    scores = jax.random.randint(key, (block_count, 14, cell_count), 0, 1 << 20) * cell_count + jnp.arange(cell_count)
    row_tile = jnp.arange(cell_count) // tile_count
    col_tile = jnp.arange(cell_count) % tile_count
    below_diag = (row_tile[None, :] > col_tile[None, :]) & (jnp.arange(14)[:, None] == 0)
    scores = jnp.where(below_diag[None], scores + (1 << 20) * cell_count, scores)
    ranking = jnp.argsort(scores, axis=-1)[..., :TP]
    tile_pairs = jnp.stack([ranking // tile_count, ranking % tile_count], axis=2)
    return tile_pairs.reshape(BX, BY, BZ, 14, 2, TP).astype(jnp.int32)


def block_levels(own_key, shape, pieces, least, largest):
    loudness = 1.0
    for axis_at, parts in pieces:
        heights = jax.random.uniform(jax.random.fold_in(jax.random.fold_in(own_key, 6), axis_at), (parts,), jnp.float32, least / len(pieces), largest / len(pieces))
        loudness = loudness * jnp.repeat(jnp.exp(heights), shape[axis_at] // parts).reshape((-1,) + (1,) * (len(shape) - 1 - axis_at))
    return loudness


def scatter_about(key, dims, width, reach, cuts=(), kind=jnp.bfloat16):
    values = width * jax.random.normal(key, dims, jnp.float32)
    if cuts:
        values = values * block_levels(key, dims, cuts, -0.22, 0.18)
    return jnp.clip(values, -reach, reach).astype(kind)


def setup_inputs(seed: int = 0) -> dict:
    key_list = jax.random.split(jax.random.key(seed), 15)
    return {
        "features": scatter_about(key_list[0], (BX, BY, BZ, A, F), 1.0, 6.0, ((0, 4), (1, 4), (2, 32))),
        "positions": jnp.clip(1.0 * jax.random.uniform(key_list[1], (BX, BY, BZ, 3, A), jnp.float32) ** block_levels(key_list[1], (BX, BY, BZ, 3, A), ((0, 4), (1, 4), (2, 32)), -0.2, 0.2), 0.0, 1.0),
        "counts": draw_counts(jax.random.fold_in(key_list[14], 71), 0),
        "pair_tiles": draw_pair_tiles(jax.random.fold_in(key_list[14], 71), 0),
        "input_weight": scatter_about(key_list[4], (F, F), F ** -0.5, 0.5),
        "radial_weight": scatter_about(key_list[5], (K, F), (K // 8) ** -0.5, 1.5),
        "radial_bias": scatter_about(key_list[6], (F,), 0.5, 3.0, (), jnp.float32),
        "filter_weight": scatter_about(key_list[7], (F, F), F ** -0.5, 0.5),
        "filter_bias": scatter_about(key_list[8], (F,), 0.5, 3.0, (), jnp.float32),
        "output_weight": scatter_about(key_list[9], (F, F), (8 * F) ** -0.5, 0.1875),
        "output_bias": scatter_about(key_list[10], (F,), 0.5, 3.0, (), jnp.float32),
        "final_weight": scatter_about(key_list[11], (F, F), F ** -0.5, 0.5),
        "final_bias": scatter_about(key_list[12], (F,), 0.5, 3.0, (), jnp.float32),
        "cotangent": scatter_about(key_list[13], (BX, BY, BZ, A, F), 0.25, 1.5, ((0, 4), (1, 4), (2, 32))),
    }


SOFTEN = 0.05
GAMMA = 40.0
LOG_TWO = math.log(2.0)

def half_shell():
    offsets = [(0, 0, 0), (1, 0, 0)]
    for step_x in (-1, 0, 1):
        offsets.append((step_x, 1, 0))
    for step_x in (-1, 0, 1):
        for step_y in (-1, 0, 1):
            offsets.append((step_x, step_y, 1))
    return offsets

def shifted_softplus(values):
    return jax.nn.softplus(values) - LOG_TWO

def pair_setup(hidden_own, hidden_other, pos_own, pos_other, present_own, present_other, tile_pair, shift_vec, self_flag, tile_size):
    tile_count = hidden_own.shape[0] // tile_size
    feat_width = hidden_own.shape[1]
    tile_left = tile_pair[0]
    tile_right = tile_pair[1]
    h_left = hidden_own.reshape(tile_count, tile_size, feat_width)[tile_left]
    h_right = hidden_other.reshape(tile_count, tile_size, feat_width)[tile_right]
    p_left = pos_own.reshape(3, tile_count, tile_size)[:, tile_left]
    p_right = pos_other.reshape(3, tile_count, tile_size)[:, tile_right]
    m_left = present_own.reshape(tile_count, tile_size)[tile_left]
    m_right = present_other.reshape(tile_count, tile_size)[tile_right]
    separation = p_right[:, :, None, :] + shift_vec[:, None, None, None] - p_left[:, :, :, None]
    distance = jnp.sqrt(lax.optimization_barrier(jnp.sum(separation * separation, axis=0)) + SOFTEN * SOFTEN)
    upper_mask = (jnp.arange(tile_size)[:, None] < jnp.arange(tile_size)[None, :]).astype(jnp.float32)
    same_tile = (tile_left == tile_right).astype(jnp.float32)[:, None, None]
    pair_keep = 1.0 - self_flag * same_tile * (1.0 - upper_mask[None])
    usable = m_left[:, :, None] * m_right[:, None, :] * pair_keep
    return (h_left, h_right, separation, distance, usable)

def filter_forward(distance, usable, weights):
    radial_weight, radial_bias, filter_weight, filter_bias = weights
    flat_dist = distance.reshape(-1)
    centres = jnp.arange(radial_weight.shape[0], dtype=jnp.float32) / radial_weight.shape[0]
    offset_gap = flat_dist[:, None] - centres[None, :]
    expansion = jnp.exp(-GAMMA * offset_gap * offset_gap)
    pre_first = jnp.dot(expansion.astype(jnp.bfloat16), radial_weight, preferred_element_type=jnp.float32) + radial_bias
    act_first = shifted_softplus(pre_first).astype(jnp.bfloat16)
    pre_second = jnp.dot(act_first, filter_weight, preferred_element_type=jnp.float32) + filter_bias
    inside = flat_dist < 1.0
    flat_usable = usable.reshape(-1)
    smooth_cut = jnp.where(inside, 0.5 * (jnp.cos(math.pi * flat_dist) + 1.0), 0.0) * flat_usable
    slope_cut = jnp.where(inside, -0.5 * math.pi * jnp.sin(math.pi * flat_dist), 0.0) * flat_usable
    return (offset_gap, expansion, pre_first, pre_second, smooth_cut, slope_cut)

def pair_forward(hidden_own, hidden_other, pos_own, pos_other, present_own, present_other, tile_pair, shift_vec, self_flag, tile_size, weights):
    h_left, h_right, separation, distance, usable = pair_setup(hidden_own, hidden_other, pos_own, pos_other, present_own, present_other, tile_pair, shift_vec, self_flag, tile_size)
    offset_gap, expansion, pre_first, pre_second, smooth_cut, slope_cut = filter_forward(distance, usable, weights)
    pair_shape = distance.shape + (hidden_own.shape[1],)
    filter_vals = (pre_second * smooth_cut[:, None]).reshape(pair_shape)
    to_left = lax.optimization_barrier(jnp.sum(filter_vals * h_right[:, None, :, :], axis=2))
    to_right = lax.optimization_barrier(jnp.sum(filter_vals * h_left[:, :, None, :], axis=1))
    return (to_left, to_right)

def pair_backward(hidden_own, hidden_other, pos_own, pos_other, present_own, present_other, grad_own, grad_other, tile_pair, shift_vec, self_flag, tile_size, weights):
    radial_weight, radial_bias, filter_weight, filter_bias = weights
    h_left, h_right, separation, distance, usable = pair_setup(hidden_own, hidden_other, pos_own, pos_other, present_own, present_other, tile_pair, shift_vec, self_flag, tile_size)
    tile_count = hidden_own.shape[0] // tile_size
    feat_width = hidden_own.shape[1]
    g_left = grad_own.reshape(tile_count, tile_size, feat_width)[tile_pair[0]]
    g_right = grad_other.reshape(tile_count, tile_size, feat_width)[tile_pair[1]]
    offset_gap, expansion, pre_first, pre_second, smooth_cut, slope_cut = filter_forward(distance, usable, weights)
    pair_shape = distance.shape + (feat_width,)
    filter_vals = (pre_second * smooth_cut[:, None]).reshape(pair_shape)
    dh_left = lax.optimization_barrier(jnp.sum(filter_vals * g_right[:, None, :, :], axis=2))
    dh_right = lax.optimization_barrier(jnp.sum(filter_vals * g_left[:, :, None, :], axis=1))
    d_filter = (g_left[:, :, None, :] * h_right[:, None, :, :] + g_right[:, None, :, :] * h_left[:, :, None, :]).reshape(-1, feat_width)
    d_second = (d_filter * smooth_cut[:, None]).astype(jnp.bfloat16)
    d_act = jnp.dot(d_second, filter_weight.T, preferred_element_type=jnp.float32)
    d_first = (d_act * jax.nn.sigmoid(pre_first)).astype(jnp.bfloat16)
    d_expand = jnp.dot(d_first, radial_weight.T, preferred_element_type=jnp.float32)
    d_dist = lax.optimization_barrier(jnp.sum(d_expand * expansion * offset_gap, axis=1)) * (-2.0 * GAMMA) + lax.optimization_barrier(jnp.sum(d_filter * pre_second, axis=1)) * slope_cut
    along = separation * (d_dist.reshape(distance.shape) / distance)[None]
    pos_left = -lax.optimization_barrier(jnp.sum(along, axis=3))
    pos_right = lax.optimization_barrier(jnp.sum(along, axis=2))
    return (dh_left, dh_right, pos_left, pos_right)

def spread(tile_index, values, tile_count):
    holder = jnp.zeros((tile_count,) + values.shape[1:], dtype=jnp.float32)
    return holder.at[tile_index].add(values).reshape(-1, values.shape[-1])

def spread_pos(tile_index, values, tile_count):
    holder = jnp.zeros((3, tile_count, values.shape[2]), dtype=jnp.float32)
    return holder.at[:, tile_index].add(values).reshape(3, -1)

def neighbour(array, step_x, step_y, step_z):
    return jnp.roll(array, (-step_x, -step_y, -step_z), axis=(0, 1, 2))

def give_back(array, step_x, step_y, step_z):
    return jnp.roll(array, (step_x, step_y, step_z), axis=(0, 1, 2))

def reference(features, positions, counts, pair_tiles, input_weight, radial_weight, radial_bias, filter_weight, filter_bias, output_weight, output_bias, final_weight, final_bias, cotangent):
    block_count = BX * BY * BZ
    tile_count = A // TILE
    weights = (radial_weight, radial_bias, filter_weight, filter_bias)
    present = (jnp.arange(A)[None, None, None, :] < counts[..., None]).astype(jnp.float32)
    hidden = jnp.dot(features.reshape(-1, F), input_weight, preferred_element_type=jnp.float32).reshape(BX, BY, BZ, A, F)
    messages = jnp.zeros((BX, BY, BZ, A, F), dtype=jnp.float32)
    for offset_index, (step_x, step_y, step_z) in enumerate(half_shell()):
        shift_vec = jnp.array([step_x, step_y, step_z], dtype=jnp.float32)
        self_flag = 1.0 if offset_index == 0 else 0.0

        def one_block(step_items):
            h_own, h_other, p_own, p_other, m_own, m_other, tile_pair = step_items
            to_left, to_right = pair_forward(h_own, h_other, p_own, p_other, m_own, m_other, tile_pair, shift_vec, self_flag, TILE, weights)
            return (spread(tile_pair[0], to_left, tile_count), spread(tile_pair[1], to_right, tile_count))
        own_part, other_part = lax.map(one_block, (hidden.reshape(block_count, A, F), neighbour(hidden, step_x, step_y, step_z).reshape(block_count, A, F), positions.reshape(block_count, 3, A), neighbour(positions, step_x, step_y, step_z).reshape(block_count, 3, A), present.reshape(block_count, A), neighbour(present, step_x, step_y, step_z).reshape(block_count, A), pair_tiles[:, :, :, offset_index].reshape(block_count, 2, TP)))
        messages = messages + own_part.reshape(BX, BY, BZ, A, F) + give_back(other_part.reshape(BX, BY, BZ, A, F), step_x, step_y, step_z)
    message_cast = messages.reshape(-1, F).astype(jnp.bfloat16)
    pre_out = jnp.dot(message_cast, output_weight, preferred_element_type=jnp.float32) + output_bias
    act_out = shifted_softplus(pre_out).astype(jnp.bfloat16)
    update = jnp.dot(act_out, final_weight, preferred_element_type=jnp.float32) + final_bias
    new_features = (features.reshape(-1, F).astype(jnp.float32) + update).astype(jnp.bfloat16)
    upstream = cotangent.reshape(-1, F)
    d_out = jnp.dot(upstream, final_weight.T, preferred_element_type=jnp.float32)
    d_pre = (d_out * jax.nn.sigmoid(pre_out)).astype(jnp.bfloat16)
    d_msg = jnp.dot(d_pre, output_weight.T, preferred_element_type=jnp.float32).reshape(BX, BY, BZ, A, F)
    d_hidden = jnp.zeros((BX, BY, BZ, A, F), dtype=jnp.float32)
    grad_pos = jnp.zeros((BX, BY, BZ, 3, A), dtype=jnp.float32)
    for offset_index, (step_x, step_y, step_z) in enumerate(half_shell()):
        shift_vec = jnp.array([step_x, step_y, step_z], dtype=jnp.float32)
        self_flag = 1.0 if offset_index == 0 else 0.0

        def back_block(step_items):
            h_own, h_other, p_own, p_other, m_own, m_other, g_own, g_other, tile_pair = step_items
            dh_left, dh_right, pos_left, pos_right = pair_backward(h_own, h_other, p_own, p_other, m_own, m_other, g_own, g_other, tile_pair, shift_vec, self_flag, TILE, weights)
            return (spread(tile_pair[0], dh_left, tile_count), spread(tile_pair[1], dh_right, tile_count), spread_pos(tile_pair[0], pos_left, tile_count), spread_pos(tile_pair[1], pos_right, tile_count))
        own_dh, other_dh, own_gp, other_gp = lax.map(back_block, (hidden.reshape(block_count, A, F), neighbour(hidden, step_x, step_y, step_z).reshape(block_count, A, F), positions.reshape(block_count, 3, A), neighbour(positions, step_x, step_y, step_z).reshape(block_count, 3, A), present.reshape(block_count, A), neighbour(present, step_x, step_y, step_z).reshape(block_count, A), d_msg.reshape(block_count, A, F), neighbour(d_msg, step_x, step_y, step_z).reshape(block_count, A, F), pair_tiles[:, :, :, offset_index].reshape(block_count, 2, TP)))
        d_hidden = d_hidden + own_dh.reshape(BX, BY, BZ, A, F) + give_back(other_dh.reshape(BX, BY, BZ, A, F), step_x, step_y, step_z)
        grad_pos = grad_pos + own_gp.reshape(BX, BY, BZ, 3, A) + give_back(other_gp.reshape(BX, BY, BZ, 3, A), step_x, step_y, step_z)
    d_hidden_cast = d_hidden.reshape(-1, F).astype(jnp.bfloat16)
    grad_features = upstream.astype(jnp.float32) + jnp.dot(d_hidden_cast, input_weight.T, preferred_element_type=jnp.float32)
    return (new_features.reshape(BX, BY, BZ, A, F), grad_features.reshape(BX, BY, BZ, A, F), -grad_pos)
```

```python
import math

import jax
import jax.numpy as jnp
import numpy as np
from jax import lax
from jax.experimental import pallas as pl
from jax.experimental.pallas import tpu as pltpu
from jax.sharding import PartitionSpec as P

TILE = 32
SOFTEN = 0.05
GAMMA = 40.0
LOG_TWO = math.log(2.0)
KAPPA = math.sqrt(GAMMA / LOG_TWO)
UNITS = 56
VMEM = 56 * 1024 * 1024


def half_shell():
    offsets = [(0, 0, 0), (1, 0, 0)]
    for step_x in (-1, 0, 1):
        offsets.append((step_x, 1, 0))
    for step_x in (-1, 0, 1):
        for step_y in (-1, 0, 1):
            offsets.append((step_x, step_y, 1))
    return offsets


SHELL = half_shell()
AROUND = [
    (sx, sy, sz)
    for sy in (0, 1, -1)
    for sx in (-1, 0, 1)
    for sz in (-1, 0, 1)
    if (sx, sy, sz) != (0, 0, 0)
]
SLOTS = [(0, 0, 0), (0, 0, 0)] + AROUND


def shell_place(offset):
    if offset in SHELL:
        return SHELL.index(offset), True
    return SHELL.index(tuple(-step for step in offset)), False


def pair_rows():
    rows = [(SLOTS[0], SLOTS[0], 0, True), (SLOTS[0], SLOTS[0], 0, False)]
    rows += [(SLOTS[0], o, *shell_place(o)) for o in AROUND]
    for side in (1, -1):
        for sx in (-1, 0, 1):
            for sz in (-1, 0, 1):
                rows.append(((0, -side, 0), (sx, side, sz), *shell_place((sx, side, sz))))
    picked = np.zeros((len(rows), 28 * 14), np.float32)
    forward = np.zeros((len(rows), 1), bool)
    for i, (reader, offset, index_k, ahead) in enumerate(rows):
        holder = reader if ahead else tuple(a + b for a, b in zip(reader, offset))
        picked[i, SLOTS.index(holder) * 14 + index_k] = 1.0
        forward[i, 0] = ahead
    return picked, forward


def whole(array):
    return pl.BlockSpec(array.shape, lambda s, *_: (0,) * array.ndim)


def exact_dot(a, b):
    return jnp.dot(a, b, precision=lax.Precision.HIGHEST)


BODY = 16
ROWS = BODY * TILE
SLABS = UNITS * TILE
BODIES = SLABS // BODY
STEP = 8
STEPS = BODIES // STEP


def last_block(step, count):
    return jnp.minimum(step, jnp.maximum((count[0] + STEP - 1) // STEP - 1, 0))


def bodies_of(step, count):
    return jnp.clip(count[0] - step * STEP, 0, STEP)


def filter_kernel(count, order, table, centres, first_w, second_w, first_b, second_b, out, out_d):
    step = pl.program_id(0)

    def one(index, carry):
        spread = [[], [], [], []]
        for j in range(BODY):
            slab = order[(step * STEP + index) * BODY + j]
            lanes = pl.ds(pl.multiple_of(slab // 128 * 128, 128), 128)
            lane = jnp.full((TILE, 128), slab % 128, jnp.int32)
            for q in range(4):
                values = table[q * TILE : (q + 1) * TILE, lanes]
                spread[q].append(jnp.take_along_axis(values, lane, axis=1, mode="promise_in_bounds"))
        x = jnp.concatenate(spread[0], axis=0) - centres[...]
        e = jnp.exp2(-(x * x))
        both = jnp.concatenate([e.astype(jnp.bfloat16), (x * e).astype(jnp.bfloat16)], axis=1)
        first = jnp.dot(both, first_w[...], preferred_element_type=jnp.float32)
        z = 1.0 + jnp.exp(first[:, 0:128] + first_b[...])
        act = jnp.log(z) - LOG_TWO
        deriv = first[:, 128:256]
        deriv = deriv - deriv * pl.reciprocal(z, approx=True)
        both2 = jnp.concatenate([act.astype(jnp.bfloat16), deriv.astype(jnp.bfloat16)], axis=1)
        second = jnp.dot(both2, second_w[...], preferred_element_type=jnp.float32)
        base = second[:, 0:128] + second_b[...]
        at_row = pl.ds(pl.multiple_of(index * ROWS, ROWS), ROWS)
        out[at_row, :] = (base * jnp.concatenate(spread[1], axis=0)).astype(jnp.bfloat16)
        out_d[at_row, :] = (
            second[:, 128:256] * jnp.concatenate(spread[2], axis=0)
            + base * jnp.concatenate(spread[3], axis=0)
        ).astype(jnp.bfloat16)
        return carry

    lax.fori_loop(0, bodies_of(step, count), one, 0)


def filters(count, order, table, first_w, second_w, first_b, second_b):
    centres = np.array(KAPPA * np.arange(128) / 128.0, np.float32)[None]
    arrays = [table, jnp.asarray(centres), first_w, second_w, first_b, second_b]
    wide = pl.BlockSpec((STEP * ROWS, 128), lambda s, n, *_: (last_block(s, n), 0))
    return pl.pallas_call(
        filter_kernel,
        grid_spec=pltpu.PrefetchScalarGridSpec(
            num_scalar_prefetch=2,
            grid=(STEPS,),
            in_specs=[whole(a) for a in arrays],
            out_specs=[wide, wide],
        ),
        out_shape=[jax.ShapeDtypeStruct((SLABS * TILE, 128), jnp.bfloat16)] * 2,
        compiler_params=pltpu.CompilerParams(vmem_limit_bytes=VMEM),
        name="pair_filters",
    )(count, order, *arrays)


def gather_kernel(starts, table, up, down):
    def one(index, carry):
        a = pl.multiple_of(starts[index], TILE)
        b = pl.multiple_of(starts[18 + index], TILE)
        o = pl.multiple_of(index * TILE, TILE)
        up[pl.ds(o, TILE), :] = table[pl.ds(a, TILE), :]
        down[pl.ds(o, TILE), :] = table[pl.ds(b, TILE), :]
        return carry

    lax.fori_loop(0, 18, one, 0)


def gather_tiles(starts, table):
    shape = (18 * TILE, 128)
    whole = pl.BlockSpec(shape, lambda s, *_: (0, 0))
    return pl.pallas_call(
        gather_kernel,
        grid_spec=pltpu.PrefetchScalarGridSpec(
            num_scalar_prefetch=1,
            grid=(1,),
            in_specs=[pl.BlockSpec(table.shape, lambda s, *_: (0, 0))],
            out_specs=[whole, whole],
        ),
        out_shape=[jax.ShapeDtypeStruct(shape, jnp.float32)] * 2,
        compiler_params=pltpu.CompilerParams(vmem_limit_bytes=VMEM),
        name="tiles_to_send",
    )(starts, table)


def softplus(values):
    return jnp.maximum(values, 0.0) + jnp.log(1.0 + jnp.exp(-jnp.abs(values)))


def nt_dot(a, b):
    return lax.dot_general(a, b, (((1,), (1,)), ((), ())), preferred_element_type=jnp.float32)


CHAINS = 4


def message_kernel(
    count, order, tiles, starts, filt, near, feats, cot, out_w, out_b, fin_w, fin_b, new, grad, *totals
):
    step = pl.program_id(0)

    @pl.when(step == 0)
    def _():
        for total in totals:
            total[...] = jnp.zeros_like(total)

    def one(index, carry):
        for j in range(BODY):
            slab = order[(step * STEP + index) * BODY + j]
            unit = slab // TILE
            h = near[pl.ds(starts[unit] + slab % TILE, 1), :]
            rows = pl.ds(pl.multiple_of(index * ROWS + j * TILE, TILE), TILE)
            own = pl.ds(pl.multiple_of(tiles[unit] * TILE, TILE), TILE)
            total = totals[j % CHAINS]
            total[own, :] = total[own, :] + filt[rows, :].astype(jnp.float32) * h
        return carry

    lax.fori_loop(0, bodies_of(step, count), one, 0)

    @pl.when(step == pl.num_programs(0) - 1)
    def _():
        cast = sum(total[...] for total in totals).astype(jnp.bfloat16)
        pre = jnp.dot(cast, out_w[...], preferred_element_type=jnp.float32) + out_b[...]
        act = (softplus(pre) - LOG_TWO).astype(jnp.bfloat16)
        update = jnp.dot(act, fin_w[...], preferred_element_type=jnp.float32) + fin_b[...]
        new[...] = (feats[...].astype(jnp.float32) + update).astype(jnp.bfloat16)
        d_out = nt_dot(cot[...], fin_w[...])
        d_pre = (d_out * jax.nn.sigmoid(pre)).astype(jnp.bfloat16)
        grad[...] = nt_dot(d_pre, out_w[...])


def back_kernel(
    count, order, tiles, starts, filt, filt_d, near, g_near, own_h, own_g, r_near, r_own, cot, in_w,
    grad, force, *totals
):
    step = pl.program_id(0)
    pushes = totals[CHAINS:]
    totals = totals[:CHAINS]

    @pl.when(step == 0)
    def _():
        for total in (*totals, *pushes):
            total[...] = jnp.zeros_like(total)

    def one(index, carry):
        slopes = []
        places = []
        for j in range(BODY):
            slab = order[(step * STEP + index) * BODY + j]
            unit = slab // TILE
            row = pl.ds(starts[unit] + slab % TILE, 1)
            h = near[row, :]
            g = g_near[row, :]
            rows = pl.ds(pl.multiple_of(index * ROWS + j * TILE, TILE), TILE)
            own = pl.ds(pl.multiple_of(tiles[unit] * TILE, TILE), TILE)
            total = totals[j % CHAINS]
            total[own, :] = total[own, :] + filt[rows, :].astype(jnp.float32) * g
            mixed = filt_d[rows, :].astype(jnp.float32) * (own_g[own, :] * h + own_h[own, :] * g)
            slopes.append(mixed.astype(jnp.bfloat16))
            places.append((own, slab))
        sums = jnp.dot(
            jnp.concatenate(slopes, axis=0),
            jnp.ones((128, 128), jnp.bfloat16),
            preferred_element_type=jnp.float32,
        )
        for j, (own, slab) in enumerate(places):
            push = pushes[j % CHAINS]
            away = r_near[pl.ds(slab, 1), :] - r_own[own, :]
            push[own, :] = push[own, :] + sums[j * TILE : (j + 1) * TILE, :] * away
        return carry

    lax.fori_loop(0, bodies_of(step, count), one, 0)

    @pl.when(step == pl.num_programs(0) - 1)
    def _():
        cast = sum(total[...] for total in totals).astype(jnp.bfloat16)
        grad[...] = cot[...].astype(jnp.float32) + nt_dot(cast, in_w[...])
        force[...] = sum(push[...] for push in pushes).T[0:8, :]


def pair_call(body, scalars, streams, arrays, outs, scratch, name):
    stream = pl.BlockSpec((STEP * ROWS, 128), lambda s, n, *_: (last_block(s, n), 0))
    return pl.pallas_call(
        body,
        grid_spec=pltpu.PrefetchScalarGridSpec(
            num_scalar_prefetch=4,
            grid=(STEPS,),
            in_specs=[stream] * len(streams) + [whole(a) for a in arrays],
            out_specs=[whole(o) for o in outs],
            scratch_shapes=[pltpu.VMEM((256, 128), jnp.float32)] * scratch,
        ),
        out_shape=outs,
        compiler_params=pltpu.CompilerParams(vmem_limit_bytes=VMEM),
        name=name,
    )(*scalars, *streams, *arrays)


def moved(x, axis, by):
    size = lax.axis_size(axis)
    return lax.ppermute(x, axis, [((i + by) % size, i) for i in range(size)])


def planes(own):
    return jnp.concatenate([moved(own, "gz", -1), own, moved(own, "gz", 1)], axis=0)


def columns(three):
    return jnp.concatenate([moved(three, "gx", -1), three, moved(three, "gx", 1)], axis=0)


def rows_around(nine, wanted):
    to_lower, to_upper = gather_tiles(wanted, nine)
    return jnp.concatenate([nine, moved(to_lower, "gy", 1), moved(to_upper, "gy", -1)], axis=0)


def block_diagonal(weight):
    zero = jnp.zeros_like(weight)
    return jnp.concatenate(
        [jnp.concatenate([weight, zero], axis=1), jnp.concatenate([zero, weight], axis=1)], axis=0
    )


def on_device(
    features,
    positions,
    counts,
    pair_tiles,
    input_weight,
    radial_weight,
    radial_bias,
    filter_weight,
    filter_bias,
    output_weight,
    output_bias,
    final_weight,
    final_bias,
    cotangent,
):
    own_features = features.reshape(256, 128)
    own_pos = positions.reshape(3, 256)
    hidden = jnp.dot(own_features, input_weight, preferred_element_type=jnp.float32)
    numbers = jnp.concatenate([counts.reshape(1), pair_tiles.reshape(56)]).astype(jnp.float32)
    meta = jnp.concatenate(
        [own_pos.reshape(6, 128), jnp.pad(numbers, (0, 71))[None], jnp.zeros((1, 128), jnp.float32)],
        axis=0,
    )
    three = planes(jnp.concatenate([hidden, meta], axis=0)[None])
    meta_three = three[:, 256:].reshape(1, 24 * 128)
    hidden_three = three[:, :256].reshape(768, 128)

    across = lax.axis_size("gy")
    along = lax.axis_size("gx")
    everyone = lax.all_to_all(
        jnp.broadcast_to(meta_three.reshape(1, 24, 128), (along * across, 24, 128)),
        ("gx", "gy"),
        0,
        0,
    ).reshape(along * across, 24 * 128)
    everyone = everyone.reshape(along * across * 3, 8 * 128)
    side = np.array(SLOTS)
    holders = (lax.axis_index("gx") + side[:, 0]) % along * across
    holders = (holders + (lax.axis_index("gy") + side[:, 1]) % across) * 3 + side[:, 2] + 1
    picker = (holders[:, None] == jnp.arange(along * across * 3)[None, :]).astype(jnp.float32)
    slots = exact_dot(picker, everyone)

    picked, forward = pair_rows()
    lists = exact_dot(picked, slots[:, 769:825].reshape(28 * 14, 4))
    lists = jnp.round(lists).astype(jnp.int32)
    mine = jnp.where(forward, lists[:, 0:2], lists[:, 2:4])
    theirs = jnp.where(forward, lists[:, 2:4], lists[:, 0:2])
    own_tiles, other_tiles = mine[:28], theirs[:28]
    column = ((side[:, 0] + 1) * 3 + side[:, 2] + 1)[:, None]
    entry = np.arange(2)[None]
    starts = jnp.where(
        (side[:, 1] == 0)[:, None],
        column * 256 + other_tiles * TILE,
        2304 + 576 * (side[:, 1:2] < 0) + (column * 2 + entry) * TILE,
    )
    wanted = (np.tile(np.arange(9), 2)[:, None] * 256 + theirs[28:] * TILE).reshape(36)

    pick_other = (other_tiles[:, :, None] == jnp.arange(8)).astype(jnp.float32)
    slot_pos = slots[:, : 6 * 128].reshape(28, 1, 3, 8, TILE)
    shift = np.repeat(np.array(SLOTS, np.float32), 2, axis=0)
    other_at = jnp.sum(pick_other[:, :, None, :, None] * slot_pos, axis=3).reshape(UNITS, 3, TILE)
    other_at = other_at + shift[:, :, None]
    same = ((own_tiles == other_tiles) & (np.arange(28) < 2)[:, None]).astype(jnp.float32)
    per_unit = jnp.stack(
        [
            own_tiles.astype(jnp.float32),
            slots[0:1, 768:769] - own_tiles * TILE,
            slots[:, 768:769] - other_tiles * TILE,
            same,
        ]
    ).reshape(4, UNITS)
    slab = np.arange(SLABS)
    per_slab = exact_dot(per_unit, (slab[None] // TILE == np.arange(UNITS)[:, None]).astype(np.float32))
    own_side = own_pos.reshape(3, 8, TILE).transpose(0, 2, 1).reshape(96, 8)
    own_at = exact_dot(
        own_side, (per_slab[0:1] == np.arange(8, dtype=np.float32)[:, None]).astype(jnp.float32)
    ).reshape(3, TILE, SLABS)
    other_row = other_at.transpose(1, 0, 2).reshape(3, 1, SLABS)
    sep = other_row - own_at
    dist = jnp.sqrt(sep[0] * sep[0] + sep[1] * sep[1] + sep[2] * sep[2] + SOFTEN * SOFTEN)
    w = jnp.asarray(slab % TILE, jnp.float32)[None]
    u = jnp.asarray(np.arange(TILE), jnp.float32)[:, None]
    reverse = jnp.asarray(slab // TILE >= 2)[None]
    drop = (per_slab[3:4] > 0.5) & jnp.where(reverse, w >= u, u >= w)
    usable = (u < per_slab[1:2]) & (w < per_slab[2:3]) & (dist < 1.0) & ~drop
    angle = math.pi * dist
    cut = jnp.where(usable, 0.5 * (jnp.cos(angle) + 1.0), 0.0)
    gain = cut * (-2.0 * GAMMA / KAPPA) / dist
    slope = jnp.where(usable, -0.5 * math.pi * jnp.sin(angle), 0.0) / dist
    table = jnp.pad(
        jnp.concatenate([KAPPA * dist, cut, gain, slope], axis=0), ((0, 0), (0, 128))
    )
    live = jnp.max(usable.astype(jnp.float32), axis=0).reshape(SLABS // 128, 128)
    until = exact_dot(live, np.triu(np.ones((128, 128), np.float32)))
    before = exact_dot(np.tril(np.ones((14, 14), np.float32), -1), until[:, 127:128])
    rank = jnp.where(live > 0.5, until + before - 1.0, -1.0).reshape(1, SLABS)
    total = jnp.sum(live).astype(jnp.int32)
    hit = rank == jnp.asarray(slab, jnp.float32)[:, None]
    order = jnp.sum(jnp.where(hit, jnp.asarray(slab)[None], 0), axis=1)
    order = jnp.where(slab < total, order, SLABS).astype(jnp.int32)
    count = ((total + BODY - 1) // BODY).reshape(1)

    filt, filt_d = filters(
        count,
        order,
        table,
        block_diagonal(radial_weight),
        block_diagonal(filter_weight),
        radial_bias[None],
        filter_bias[None],
    )
    near = rows_around(columns(hidden_three), wanted)
    cot = cotangent.reshape(256, 128)
    scalars = (
        count,
        order,
        jnp.pad(own_tiles.reshape(UNITS), (0, 8)),
        jnp.pad(starts.reshape(UNITS), (0, 8)).astype(jnp.int32),
    )
    new_features, d_msg = pair_call(
        message_kernel,
        scalars,
        [filt],
        [
            near,
            own_features,
            cot,
            output_weight,
            output_bias[None],
            final_weight,
            final_bias[None],
        ],
        [
            jax.ShapeDtypeStruct((256, 128), jnp.bfloat16),
            jax.ShapeDtypeStruct((256, 128), jnp.float32),
        ],
        CHAINS,
        "messages_and_update",
    )
    g_near = rows_around(columns(planes(d_msg)), wanted)
    r_near = jnp.pad(other_at.transpose(0, 2, 1).reshape(SLABS, 3), ((0, 8), (0, 125)))
    r_own = jnp.pad(own_pos.T, ((0, 0), (0, 125)))
    grad_features, force = pair_call(
        back_kernel,
        scalars,
        [filt, filt_d],
        [near, g_near, hidden, d_msg, r_near, r_own, cot, input_weight],
        [
            jax.ShapeDtypeStruct((256, 128), jnp.float32),
            jax.ShapeDtypeStruct((8, 256), jnp.float32),
        ],
        2 * CHAINS,
        "pair_gradients",
    )
    return (
        new_features.reshape(1, 1, 1, 256, 128),
        grad_features.reshape(1, 1, 1, 256, 128),
        force[:3].reshape(1, 1, 1, 3, 256),
    )


def solution(mesh):
    block = P("gx", "gy", "gz", None, None)
    return jax.shard_map(
        on_device,
        mesh=mesh,
        in_specs=(
            block,
            block,
            P("gx", "gy", "gz"),
            P("gx", "gy", "gz", None, None, None),
            *([P()] * 9),
            block,
        ),
        out_specs=(block, block, block),
        check_vma=False,
    )
```

```python
import math

import jax
import jax.numpy as jnp
import numpy as np
from jax import lax
from jax.experimental import pallas as pl
from jax.experimental.pallas import tpu as pltpu
from jax.sharding import PartitionSpec as P

TILE = 32
SOFTEN = 0.05
GAMMA = 40.0
LOG_TWO = math.log(2.0)
KAPPA = math.sqrt(GAMMA / LOG_TWO)
UNITS = 56
VMEM = 56 * 1024 * 1024


def half_shell():
    offsets = [(0, 0, 0), (1, 0, 0)]
    for step_x in (-1, 0, 1):
        offsets.append((step_x, 1, 0))
    for step_x in (-1, 0, 1):
        for step_y in (-1, 0, 1):
            offsets.append((step_x, step_y, 1))
    return offsets


SHELL = half_shell()
AROUND = [
    (sx, sy, sz)
    for sy in (0, 1, -1)
    for sx in (-1, 0, 1)
    for sz in (-1, 0, 1)
    if (sx, sy, sz) != (0, 0, 0)
]
SLOTS = [(0, 0, 0), (0, 0, 0)] + AROUND


def shell_place(offset):
    if offset in SHELL:
        return SHELL.index(offset), True
    return SHELL.index(tuple(-step for step in offset)), False


def pair_rows():
    rows = [(SLOTS[0], SLOTS[0], 0, True), (SLOTS[0], SLOTS[0], 0, False)]
    rows += [(SLOTS[0], o, *shell_place(o)) for o in AROUND]
    for side in (1, -1):
        for sx in (-1, 0, 1):
            for sz in (-1, 0, 1):
                rows.append(((0, -side, 0), (sx, side, sz), *shell_place((sx, side, sz))))
    picked = np.zeros((len(rows), 28 * 14), np.float32)
    forward = np.zeros((len(rows), 1), bool)
    for i, (reader, offset, index_k, ahead) in enumerate(rows):
        holder = reader if ahead else tuple(a + b for a, b in zip(reader, offset))
        picked[i, SLOTS.index(holder) * 14 + index_k] = 1.0
        forward[i, 0] = ahead
    return picked, forward


def whole(array):
    return pl.BlockSpec(array.shape, lambda s, *_: (0,) * array.ndim)


def exact_dot(a, b):
    return jnp.dot(a, b, precision=lax.Precision.HIGHEST)


BODY = 64
ROWS = BODY * TILE
SLABS = UNITS * TILE
NINE = 9 * 256
AROUND_ROWS = NINE + 2 * 18 * TILE
BODIES = SLABS // BODY
STEP = 2
STEPS = BODIES // STEP


def last_block(step, count):
    return jnp.minimum(step, jnp.maximum((count[0] + STEP - 1) // STEP - 1, 0))


def bodies_of(step, count):
    return jnp.clip(count[0] - step * STEP, 0, STEP)


def filter_kernel(count, order, table, centres, first_w, second_w, first_b, second_b, out, out_d):
    step = pl.program_id(0)

    def one(index, carry):
        spread = [[], [], [], []]
        for j in range(BODY):
            slab = order[(step * STEP + index) * BODY + j]
            lanes = pl.ds(pl.multiple_of(slab // 128 * 128, 128), 128)
            lane = jnp.full((TILE, 128), slab % 128, jnp.int32)
            for q in range(4):
                values = table[q * TILE : (q + 1) * TILE, lanes]
                spread[q].append(jnp.take_along_axis(values, lane, axis=1, mode="promise_in_bounds"))
        x = jnp.concatenate(spread[0], axis=0) - centres[...]
        e = jnp.exp2(-(x * x))
        both = jnp.concatenate([e.astype(jnp.bfloat16), (x * e).astype(jnp.bfloat16)], axis=1)
        first = jnp.dot(both, first_w[...], preferred_element_type=jnp.float32)
        z = 1.0 + jnp.exp(first[:, 0:128] + first_b[...])
        act = jnp.log(z) - LOG_TWO
        deriv = first[:, 128:256]
        deriv = deriv - deriv * pltpu.reciprocal(z, approx=True)
        both2 = jnp.concatenate([act.astype(jnp.bfloat16), deriv.astype(jnp.bfloat16)], axis=1)
        second = jnp.dot(both2, second_w[...], preferred_element_type=jnp.float32)
        base = second[:, 0:128] + second_b[...]
        at_row = pl.ds(pl.multiple_of(index * ROWS, ROWS), ROWS)
        out[at_row, :] = (base * jnp.concatenate(spread[1], axis=0)).astype(jnp.bfloat16)
        out_d[at_row, :] = (
            second[:, 128:256] * jnp.concatenate(spread[2], axis=0)
            + base * jnp.concatenate(spread[3], axis=0)
        ).astype(jnp.bfloat16)
        return carry

    lax.fori_loop(0, bodies_of(step, count), one, 0)


def filters(count, order, table, first_w, second_w, first_b, second_b):
    centres = np.array(KAPPA * np.arange(128) / 128.0, np.float32)[None]
    arrays = [table, jnp.asarray(centres), first_w, second_w, first_b, second_b]
    wide = pl.BlockSpec((STEP * ROWS, 128), lambda s, n, *_: (last_block(s, n), 0))
    return pl.pallas_call(
        filter_kernel,
        grid_spec=pltpu.PrefetchScalarGridSpec(
            num_scalar_prefetch=2,
            grid=(STEPS,),
            in_specs=[whole(a) for a in arrays],
            out_specs=[wide, wide],
        ),
        out_shape=[jax.ShapeDtypeStruct((SLABS * TILE, 128), jnp.bfloat16)] * 2,
        compiler_params=pltpu.CompilerParams(vmem_limit_bytes=VMEM),
        name="pair_filters",
    )(count, order, *arrays)


def laid_end_to_end(pieces, held):
    row = 0
    for piece in pieces:
        held[row : row + piece.shape[0], :] = piece[...]
        row += piece.shape[0]


def gather_kernel(starts, one_side, middle, other_side, near, far, held):
    laid_end_to_end((one_side, middle, other_side), held)

    def one(index, carry):
        a = pl.multiple_of(starts[index], TILE)
        b = pl.multiple_of(starts[18 + index], TILE)
        o = pl.multiple_of(index * TILE, TILE)
        near[pl.ds(o, TILE), :] = held[pl.ds(a, TILE), :]
        far[pl.ds(o, TILE), :] = held[pl.ds(b, TILE), :]
        return carry

    lax.fori_loop(0, 18, one, 0)


def gather_tiles(starts, pieces):
    shape = (18 * TILE, 128)
    outs = [jax.ShapeDtypeStruct(shape, jnp.float32)] * 2
    return pl.pallas_call(
        gather_kernel,
        grid_spec=pltpu.PrefetchScalarGridSpec(
            num_scalar_prefetch=1,
            grid=(1,),
            in_specs=[whole(p) for p in pieces],
            out_specs=[whole(o) for o in outs],
            scratch_shapes=[pltpu.VMEM((NINE, 128), jnp.float32)],
        ),
        out_shape=outs,
        compiler_params=pltpu.CompilerParams(vmem_limit_bytes=VMEM),
        name="tiles_to_send",
    )(starts, *pieces)


def softplus(values):
    return jnp.maximum(values, 0.0) + jnp.log(1.0 + jnp.exp(-jnp.abs(values)))


def nt_dot(a, b):
    return lax.dot_general(a, b, (((1,), (1,)), ((), ())), preferred_element_type=jnp.float32)


CHAINS = 4


def message_kernel(
    count, order, tiles, starts, filt, p0, p1, p2, p3, p4, feats, cot, out_w, out_b, fin_w, fin_b,
    new, grad, near, *totals
):
    step = pl.program_id(0)

    @pl.when(step == 0)
    def _():
        laid_end_to_end((p0, p1, p2, p3, p4), near)
        for total in totals:
            total[...] = jnp.zeros_like(total)

    def one(index, carry):
        for j in range(BODY):
            slab = order[(step * STEP + index) * BODY + j]
            unit = slab // TILE
            h = near[pl.ds(starts[unit] + slab % TILE, 1), :]
            rows = pl.ds(pl.multiple_of(index * ROWS + j * TILE, TILE), TILE)
            own = pl.ds(pl.multiple_of(tiles[unit] * TILE, TILE), TILE)
            total = totals[j % CHAINS]
            total[own, :] = total[own, :] + filt[rows, :].astype(jnp.float32) * h
        return carry

    lax.fori_loop(0, bodies_of(step, count), one, 0)

    @pl.when(step == pl.num_programs(0) - 1)
    def _():
        cast = sum(total[...] for total in totals).astype(jnp.bfloat16)
        pre = jnp.dot(cast, out_w[...], preferred_element_type=jnp.float32) + out_b[...]
        act = (softplus(pre) - LOG_TWO).astype(jnp.bfloat16)
        update = jnp.dot(act, fin_w[...], preferred_element_type=jnp.float32) + fin_b[...]
        new[...] = (feats[...].astype(jnp.float32) + update).astype(jnp.bfloat16)
        d_out = nt_dot(cot[...], fin_w[...])
        d_pre = (d_out * jax.nn.sigmoid(pre)).astype(jnp.bfloat16)
        grad[...] = nt_dot(d_pre, out_w[...])


def back_kernel(
    count, order, tiles, starts, filt, filt_d, h0, h1, h2, h3, h4, g0, g1, g2, g3, g4, own_h, own_g,
    r_near, r_own, cot, in_w, grad, force, near, g_near, *totals
):
    step = pl.program_id(0)
    pushes = totals[CHAINS:]
    totals = totals[:CHAINS]

    @pl.when(step == 0)
    def _():
        laid_end_to_end((h0, h1, h2, h3, h4), near)
        laid_end_to_end((g0, g1, g2, g3, g4), g_near)
        for total in (*totals, *pushes):
            total[...] = jnp.zeros_like(total)

    def one(index, carry):
        slopes = []
        places = []
        for j in range(BODY):
            slab = order[(step * STEP + index) * BODY + j]
            unit = slab // TILE
            row = pl.ds(starts[unit] + slab % TILE, 1)
            h = near[row, :]
            g = g_near[row, :]
            rows = pl.ds(pl.multiple_of(index * ROWS + j * TILE, TILE), TILE)
            own = pl.ds(pl.multiple_of(tiles[unit] * TILE, TILE), TILE)
            total = totals[j % CHAINS]
            total[own, :] = total[own, :] + filt[rows, :].astype(jnp.float32) * g
            mixed = filt_d[rows, :].astype(jnp.float32) * (own_g[own, :] * h + own_h[own, :] * g)
            slopes.append(mixed.astype(jnp.bfloat16))
            places.append((own, slab))
        sums = jnp.dot(
            jnp.concatenate(slopes, axis=0),
            jnp.ones((128, 128), jnp.bfloat16),
            preferred_element_type=jnp.float32,
        )
        for j, (own, slab) in enumerate(places):
            push = pushes[j % CHAINS]
            away = r_near[pl.ds(slab, 1), :] - r_own[own, :]
            push[own, :] = push[own, :] + sums[j * TILE : (j + 1) * TILE, :] * away
        return carry

    lax.fori_loop(0, bodies_of(step, count), one, 0)

    @pl.when(step == pl.num_programs(0) - 1)
    def _():
        cast = sum(total[...] for total in totals).astype(jnp.bfloat16)
        grad[...] = cot[...].astype(jnp.float32) + nt_dot(cast, in_w[...])
        force[...] = sum(push[...] for push in pushes).T[0:8, :]


def pair_call(body, scalars, streams, arrays, outs, tables, scratch, name):
    stream = pl.BlockSpec((STEP * ROWS, 128), lambda s, n, *_: (last_block(s, n), 0))
    return pl.pallas_call(
        body,
        grid_spec=pltpu.PrefetchScalarGridSpec(
            num_scalar_prefetch=4,
            grid=(STEPS,),
            in_specs=[stream] * len(streams) + [whole(a) for a in arrays],
            out_specs=[whole(o) for o in outs],
            scratch_shapes=[pltpu.VMEM((AROUND_ROWS, 128), jnp.float32)] * tables
            + [pltpu.VMEM((256, 128), jnp.float32)] * scratch,
        ),
        out_shape=outs,
        compiler_params=pltpu.CompilerParams(vmem_limit_bytes=VMEM),
        name=name,
    )(*scalars, *streams, *arrays)


def swapped(to_far, to_near, axis):
    size = lax.axis_size(axis)
    near = [(i, i ^ 1) for i in range(size)]
    far = [(i, ((i ^ 1) + 2 * (2 * (i % 2) - 1)) % size) for i in range(size)]
    from_far = lax.ppermute(to_far, axis, far)
    return lax.ppermute(to_near, axis, near), from_far


def place_of(steps, axis):
    return 1 - steps * (1 - 2 * (lax.axis_index(axis) % 2))


def planes(own):
    near, far = swapped(own, own, "gz")
    return jnp.concatenate([near, own, far], axis=0)


def columns(three):
    near, far = swapped(three, three, "gx")
    return [near, three, far]


def block_diagonal(weight):
    zero = jnp.zeros_like(weight)
    return jnp.concatenate(
        [jnp.concatenate([weight, zero], axis=1), jnp.concatenate([zero, weight], axis=1)], axis=0
    )


def on_device(
    features,
    positions,
    counts,
    pair_tiles,
    input_weight,
    radial_weight,
    radial_bias,
    filter_weight,
    filter_bias,
    output_weight,
    output_bias,
    final_weight,
    final_bias,
    cotangent,
):
    own_features = features.reshape(256, 128)
    own_pos = positions.reshape(3, 256)
    hidden = jnp.dot(own_features, input_weight, preferred_element_type=jnp.float32)
    numbers = jnp.concatenate([counts.reshape(1), pair_tiles.reshape(56)]).astype(jnp.float32)
    meta = jnp.concatenate(
        [own_pos.reshape(6, 128), jnp.pad(numbers, (0, 71))[None], jnp.zeros((1, 128), jnp.float32)],
        axis=0,
    )
    three = planes(jnp.concatenate([hidden, meta], axis=0)[None])
    meta_three = three[:, 256:].reshape(1, 24 * 128)
    hidden_three = three[:, :256].reshape(768, 128)

    across = lax.axis_size("gy")
    along = lax.axis_size("gx")
    everyone = lax.all_to_all(
        jnp.broadcast_to(meta_three.reshape(1, 24, 128), (along * across, 24, 128)),
        ("gx", "gy"),
        0,
        0,
    ).reshape(along * across, 24 * 128)
    everyone = everyone.reshape(along * across * 3, 8 * 128)
    side = np.array(SLOTS)
    holders = (lax.axis_index("gx") + side[:, 0]) % along * across
    holders = (holders + (lax.axis_index("gy") + side[:, 1]) % across) * 3
    holders = holders + place_of(side[:, 2], "gz")
    picker = (holders[:, None] == jnp.arange(along * across * 3)[None, :]).astype(jnp.float32)
    slots = exact_dot(picker, everyone)

    picked, forward = pair_rows()
    lists = exact_dot(picked, slots[:, 769:825].reshape(28 * 14, 4))
    lists = jnp.round(lists).astype(jnp.int32)
    mine = jnp.where(forward, lists[:, 0:2], lists[:, 2:4])
    theirs = jnp.where(forward, lists[:, 2:4], lists[:, 0:2])
    own_tiles, other_tiles = mine[:28], theirs[:28]
    column = (place_of(side[:, 0], "gx") * 3 + place_of(side[:, 2], "gz"))[:, None]
    listed = ((side[:, 0] + 1) * 3 + side[:, 2] + 1)[:, None]
    entry = np.arange(2)[None]
    starts = jnp.where(
        (side[:, 1] == 0)[:, None],
        column * 256 + other_tiles * TILE,
        NINE + 288 * place_of(side[:, 1:2], "gy") + (listed * 2 + entry) * TILE,
    )
    sent = np.array([(sx, sz) for sx in (-1, 0, 1) for sz in (-1, 0, 1)])
    sent_column = (place_of(sent[:, 0], "gx") * 3 + place_of(sent[:, 1], "gz"))[:, None]
    wanted = sent_column * 256 + theirs[28:].reshape(2, 9, 2) * TILE
    lower, upper = wanted[0].reshape(18), wanted[1].reshape(18)
    even = lax.axis_index("gy") % 2 == 0
    wanted = jnp.concatenate([jnp.where(even, upper, lower), jnp.where(even, lower, upper)])

    pick_other = (other_tiles[:, :, None] == jnp.arange(8)).astype(jnp.float32)
    slot_pos = slots[:, : 6 * 128].reshape(28, 1, 3, 8, TILE)
    shift = np.repeat(np.array(SLOTS, np.float32), 2, axis=0)
    other_at = jnp.sum(pick_other[:, :, None, :, None] * slot_pos, axis=3).reshape(UNITS, 3, TILE)
    other_at = other_at + shift[:, :, None]
    same = ((own_tiles == other_tiles) & (np.arange(28) < 2)[:, None]).astype(jnp.float32)
    per_unit = jnp.stack(
        [
            own_tiles.astype(jnp.float32),
            slots[0:1, 768:769] - own_tiles * TILE,
            slots[:, 768:769] - other_tiles * TILE,
            same,
        ]
    ).reshape(4, UNITS)
    slab = np.arange(SLABS)
    per_slab = exact_dot(per_unit, (slab[None] // TILE == np.arange(UNITS)[:, None]).astype(np.float32))
    own_side = own_pos.reshape(3, 8, TILE).transpose(0, 2, 1).reshape(96, 8)
    own_at = exact_dot(
        own_side, (per_slab[0:1] == np.arange(8, dtype=np.float32)[:, None]).astype(jnp.float32)
    ).reshape(3, TILE, SLABS)
    other_row = other_at.transpose(1, 0, 2).reshape(3, 1, SLABS)
    sep = other_row - own_at
    dist = jnp.sqrt(sep[0] * sep[0] + sep[1] * sep[1] + sep[2] * sep[2] + SOFTEN * SOFTEN)
    w = jnp.asarray(slab % TILE, jnp.float32)[None]
    u = jnp.asarray(np.arange(TILE), jnp.float32)[:, None]
    reverse = jnp.asarray(slab // TILE >= 2)[None]
    drop = (per_slab[3:4] > 0.5) & jnp.where(reverse, w >= u, u >= w)
    usable = (u < per_slab[1:2]) & (w < per_slab[2:3]) & (dist < 1.0) & ~drop
    angle = math.pi * dist
    cut = jnp.where(usable, 0.5 * (jnp.cos(angle) + 1.0), 0.0)
    gain = cut * (-2.0 * GAMMA / KAPPA) / dist
    slope = jnp.where(usable, -0.5 * math.pi * jnp.sin(angle), 0.0) / dist
    table = jnp.pad(
        jnp.concatenate([KAPPA * dist, cut, gain, slope], axis=0), ((0, 0), (0, 128))
    )
    live = jnp.max(usable.astype(jnp.float32), axis=0).reshape(SLABS // 128, 128)
    until = exact_dot(live, np.triu(np.ones((128, 128), np.float32)))
    before = exact_dot(np.tril(np.ones((14, 14), np.float32), -1), until[:, 127:128])
    rank = jnp.where(live > 0.5, until + before - 1.0, -1.0).reshape(1, SLABS)
    total = jnp.sum(live).astype(jnp.int32)
    hit = rank == jnp.asarray(slab, jnp.float32)[:, None]
    order = jnp.sum(jnp.where(hit, jnp.asarray(slab)[None], 0), axis=1)
    order = jnp.where(slab < total, order, SLABS).astype(jnp.int32)
    count = ((total + BODY - 1) // BODY).reshape(1)

    near_x = columns(hidden_three)
    to_near, to_far, count = lax.optimization_barrier((*gather_tiles(wanted, near_x), count))
    near = [*near_x, *swapped(to_far, to_near, "gy")]
    filt, filt_d = filters(
        count,
        order,
        table,
        block_diagonal(radial_weight),
        block_diagonal(filter_weight),
        radial_bias[None],
        filter_bias[None],
    )
    cot = cotangent.reshape(256, 128)
    scalars = (
        count,
        order,
        jnp.pad(own_tiles.reshape(UNITS), (0, 8)),
        jnp.pad(starts.reshape(UNITS), (0, 8)).astype(jnp.int32),
    )
    new_features, d_msg = pair_call(
        message_kernel,
        scalars,
        [filt],
        [
            *near,
            own_features,
            cot,
            output_weight,
            output_bias[None],
            final_weight,
            final_bias[None],
        ],
        [
            jax.ShapeDtypeStruct((256, 128), jnp.bfloat16),
            jax.ShapeDtypeStruct((256, 128), jnp.float32),
        ],
        1,
        CHAINS,
        "messages_and_update",
    )
    g_x = columns(planes(d_msg))
    to_near, to_far = gather_tiles(wanted, g_x)
    g_near = [*g_x, *swapped(to_far, to_near, "gy")]
    r_near = jnp.pad(other_at.transpose(0, 2, 1).reshape(SLABS, 3), ((0, 8), (0, 125)))
    r_own = jnp.pad(own_pos.T, ((0, 0), (0, 125)))
    grad_features, force = pair_call(
        back_kernel,
        scalars,
        [filt, filt_d],
        [*near, *g_near, hidden, d_msg, r_near, r_own, cot, input_weight],
        [
            jax.ShapeDtypeStruct((256, 128), jnp.float32),
            jax.ShapeDtypeStruct((8, 256), jnp.float32),
        ],
        2,
        2 * CHAINS,
        "pair_gradients",
    )
    return (
        new_features.reshape(1, 1, 1, 256, 128),
        grad_features.reshape(1, 1, 1, 256, 128),
        force[:3].reshape(1, 1, 1, 3, 256),
    )


def solution(mesh):
    block = P("gx", "gy", "gz", None, None)
    return jax.shard_map(
        on_device,
        mesh=mesh,
        in_specs=(
            block,
            block,
            P("gx", "gy", "gz"),
            P("gx", "gy", "gz", None, None, None),
            *([P()] * 9),
            block,
        ),
        out_specs=(block, block, block),
        check_vma=False,
    )
```

```python
import math

import jax
import jax.numpy as jnp
import numpy as np
from jax import lax
from jax.experimental import pallas as pl
from jax.experimental.pallas import tpu as pltpu
from jax.sharding import PartitionSpec as P

TILE = 32
SOFTEN = 0.05
GAMMA = 40.0
LOG_TWO = math.log(2.0)
KAPPA = math.sqrt(GAMMA / LOG_TWO)
UNITS = 56
VMEM = 56 * 1024 * 1024


def half_shell():
    offsets = [(0, 0, 0), (1, 0, 0)]
    for step_x in (-1, 0, 1):
        offsets.append((step_x, 1, 0))
    for step_x in (-1, 0, 1):
        for step_y in (-1, 0, 1):
            offsets.append((step_x, step_y, 1))
    return offsets


SHELL = half_shell()
AROUND = [
    (sx, sy, sz)
    for sy in (0, 1, -1)
    for sx in (-1, 0, 1)
    for sz in (-1, 0, 1)
    if (sx, sy, sz) != (0, 0, 0)
]
SLOTS = [(0, 0, 0), (0, 0, 0)] + AROUND


def shell_place(offset):
    if offset in SHELL:
        return SHELL.index(offset), True
    return SHELL.index(tuple(-step for step in offset)), False


SLOT_ROWS = 32
LIST_ROWS = 56
SENT = [(sx, sz) for sx in (-1, 0, 1) for sz in (-1, 0, 1)]


def list_selectors(sides):
    rows = {0: (SLOTS[0], SLOTS[0], 0, True), 1: (SLOTS[0], SLOTS[0], 0, False)}
    for i, offset in enumerate(AROUND):
        rows[2 + i] = (SLOTS[0], offset, *shell_place(offset))
    for j, side in enumerate(sides):
        for m, (sx, sz) in enumerate(SENT):
            offset = (sx, side, sz)
            rows[SLOT_ROWS + 9 * j + m] = ((0, -side, 0), offset, *shell_place(offset))
    holders = np.zeros((LIST_ROWS, SLOT_ROWS), np.float32)
    lanes = np.zeros((4, LIST_ROWS, 128), np.float32)
    for i, (reader, offset, index_k, ahead) in rows.items():
        holder = reader if ahead else tuple(a + b for a, b in zip(reader, offset))
        holders[i, SLOTS.index(holder)] = 1.0
        for q in range(4):
            lanes[q, i, 1 + 4 * index_k + (q if ahead else (q + 2) % 4)] = 1.0
    return holders, lanes


def list_bases():
    def place_of(steps, odd):
        return 1 - steps * (1 - 2 * odd)

    def rows(odd_x, odd_y, odd_z):
        bases = np.zeros((LIST_ROWS, 3), np.float32)
        for i, (sx, sy, sz) in enumerate(SLOTS):
            if sy == 0:
                first = (place_of(sx, odd_x) * 3 + place_of(sz, odd_z)) * 256
                bases[i] = first, first, TILE
            else:
                listed = (sx + 1) * 3 + sz + 1
                first = NINE + 576 * place_of(sy, odd_y) // 2 + listed * 2 * TILE
                bases[i] = first, first + TILE, 0
        for i, (sx, sz) in enumerate(SENT):
            first = (place_of(sx, odd_x) * 3 + place_of(sz, odd_z)) * 256
            for at in (SLOT_ROWS + i, SLOT_ROWS + 9 + i):
                bases[at] = first, first, TILE
        return bases

    even = rows(0, 0, 0)
    return np.stack([even, rows(1, 0, 0) - even, rows(0, 1, 0) - even, rows(0, 0, 1) - even])


def whole(array):
    return pl.BlockSpec(array.shape, lambda s, *_: (0,) * array.ndim)


def exact_dot(a, b):
    return jnp.dot(a, b, precision=lax.Precision.HIGHEST)


BODY = 64
ROWS = BODY * TILE
SLABS = UNITS * TILE
NINE = 9 * 256
AROUND_ROWS = NINE + 2 * 18 * TILE
BODIES = SLABS // BODY
WIDE = 2 * SLOT_ROWS * TILE
IDLE = 28 * TILE
STEP = 2
STEPS = BODIES // STEP


def prepare_kernel(
    where, everyone, holders, lanes, bases, side, shift, own_side, units,
    table, order, own_rows, other_rows, lists, count, at_unit
):
    f32 = jnp.float32
    odd = [where[a] & 1 for a in range(3)]
    device = ((where[0] + side[:, 0:1]) & 3) * 4 + ((where[1] + side[:, 1:2]) & 3)
    device = device * 3 + 1 - side[:, 2:3] * (1 - 2 * odd[2])
    device = jnp.where(side[:, 3:4] > 0, device, -1)
    devices = lax.broadcasted_iota(jnp.int32, (SLOT_ROWS, 48), 1)
    slots = exact_dot(jnp.where(devices == device, 1.0, 0.0), everyone[...])
    numbers = slots[:, 768:896]
    rows = exact_dot(holders[odd[1]], numbers)
    tiles = [jnp.sum(rows * lanes[odd[1], q], axis=1, keepdims=True) for q in range(4)]
    lane = lax.broadcasted_iota(jnp.int32, (LIST_ROWS, 128), 1)
    base = bases[0]
    for a in range(3):
        base = base + bases[1 + a] * odd[a].astype(f32)
    place = [base[:, n : n + 1] + base[:, 2:3] * tiles[2 + n] for n in range(2)]
    listed = jnp.where(lane < 1, tiles[0], jnp.where(lane < 2, tiles[1], place[1]))
    listed = jnp.where(lane == 2, place[0], listed)
    lists[...] = jnp.round(listed).astype(jnp.int32)

    slot = lax.broadcasted_iota(jnp.int32, (SLOT_ROWS, 1), 0)
    halves = []
    for n in range(2):
        own = tiles[n][0:SLOT_ROWS]
        other = tiles[2 + n][0:SLOT_ROWS]
        at = []
        for c in range(3):
            acc = jnp.zeros((SLOT_ROWS, TILE), f32)
            for t in range(8):
                first = c * 256 + t * TILE
                acc = acc + jnp.where(jnp.abs(other - t) < 0.5, slots[:, first : first + TILE], 0.0)
            at.append(acc + shift[:, c : c + 1])
        same = jnp.where((jnp.abs(own - other) < 0.5) & (slot < 2), 1.0, 0.0)
        own_left = numbers[0:1, 0:1] - own * TILE
        other_left = numbers[:, 0:1] - other * TILE
        rest = jnp.where(lane[0:SLOT_ROWS, 0:TILE] == 0, own, 0.0)
        for q, value in enumerate((own_left, other_left, same, place[n][0:SLOT_ROWS] * (1.0 / TILE))):
            rest = jnp.where(lane[0:SLOT_ROWS, 0:TILE] == q + 1, value, rest)
        halves.append(jnp.concatenate([*at, rest], axis=1))
    per_unit = jnp.concatenate(halves, axis=0)
    at_unit[...] = per_unit
    per_slab = jnp.dot(in_thirds(per_unit.T), units[...], preferred_element_type=f32)

    slab = lax.broadcasted_iota(jnp.int32, (TILE, WIDE), 1)
    u = lax.broadcasted_iota(jnp.int32, (TILE, WIDE), 0)
    w = slab & (TILE - 1)
    own_tile = per_slab[96:97]
    eight = lax.broadcasted_iota(jnp.int32, (8, WIDE), 0).astype(f32)
    chosen = jnp.where(jnp.abs(own_tile - eight) < 0.5, 1.0, 0.0).astype(jnp.bfloat16)
    own_at = jnp.dot(
        in_thirds(own_side[...]), jnp.concatenate([chosen] * 3, axis=0), preferred_element_type=f32
    )
    square = jnp.full((TILE, WIDE), SOFTEN * SOFTEN, f32)
    for c in range(3):
        part = slice(c * TILE, (c + 1) * TILE)
        other_at = jnp.sum(jnp.where(u == w, per_slab[part], 0.0), axis=0, keepdims=True)
        sep = other_at - own_at[part]
        square = square + sep * sep
    dist = jnp.sqrt(square)
    reverse = ((slab >> 5) & (SLOT_ROWS - 1)) == 1
    away = jnp.where(reverse, u - w, w - u)
    drop = (per_slab[99:100] > 0.5) & (away <= 0)
    fits = (u.astype(f32) < per_slab[97:98]) & (w.astype(f32) < per_slab[98:99])
    usable = fits & (dist < 1.0) & jnp.logical_not(drop)
    angle = math.pi * dist
    near = 1.0 / dist
    cut = jnp.where(usable, 0.5 * (jnp.cos(angle) + 1.0), 0.0)
    table[0:TILE, :] = KAPPA * dist
    table[TILE : 2 * TILE, :] = cut
    table[2 * TILE : 3 * TILE, :] = cut * (-2.0 * GAMMA / KAPPA) * near
    table[3 * TILE : 4 * TILE, :] = jnp.where(usable, -0.5 * math.pi * jnp.sin(angle), 0.0) * near

    live = jnp.max(jnp.where(usable, 1.0, 0.0), axis=0, keepdims=True)
    blocks = WIDE // 128
    live = jnp.concatenate([live[:, b * 128 : (b + 1) * 128] for b in range(blocks)], axis=0)
    row = lax.broadcasted_iota(jnp.int32, (128, 128), 0)
    col = lax.broadcasted_iota(jnp.int32, (128, 128), 1)
    upto = jnp.where(row <= col, 1.0, 0.0).astype(jnp.bfloat16)
    until = jnp.dot(live.astype(jnp.bfloat16), upto, preferred_element_type=f32)
    sums = jnp.broadcast_to(until[:, 127:128], (blocks, 128)).astype(jnp.bfloat16)
    below = jnp.where(row > col, 1.0, 0.0).astype(jnp.bfloat16)[0:blocks, 0:blocks]
    before = jnp.dot(below, sums, preferred_element_type=f32)
    rank = jnp.where(live > 0.5, until + before - 1.0, -1.0)
    total = before[blocks - 1 : blocks, :] + until[blocks - 1 : blocks, 127:128]
    bodies = jnp.floor((total + (BODY - 1.0)) * (1.0 / BODY))
    count[...] = jnp.broadcast_to(bodies, (8, 128)).astype(jnp.int32)
    target = lax.broadcasted_iota(jnp.int32, (SLABS, 256), 0).astype(f32)
    names_row = lax.broadcasted_iota(jnp.int32, (8, 256), 0)
    names_lane = lax.broadcasted_iota(jnp.int32, (8, 256), 1)
    found = jnp.zeros((8, SLABS), f32)
    for b in range(blocks // 2):
        wide_rank = jnp.concatenate([rank[2 * b : 2 * b + 1], rank[2 * b + 1 : 2 * b + 2]], axis=1)
        hit = jnp.where(target == wide_rank, 1.0, 0.0).astype(jnp.bfloat16)
        names = jnp.where(names_row == 0, b * 8 + (names_lane >> 5), names_lane & (TILE - 1))
        names = jnp.where(names_row == 2, 1, names).astype(f32)
        part = slice(b * 256, (b + 1) * 256)
        names = jnp.where(names_row == 3, per_slab[96:97, part], names)
        names = jnp.where(names_row == 4, per_slab[100:101, part], names)
        found = found + nt_dot(names.astype(jnp.bfloat16), hit)
    named = jnp.where(found[2:3] > 0.5, found[0:1] * TILE + found[1:2], 1.0 * IDLE)
    order[...] = jnp.round(named).astype(jnp.int32)
    own_rows[...] = jnp.round(found[3:4] * TILE).astype(jnp.int32)
    other_rows[...] = jnp.round(found[4:5] * TILE + found[1:2]).astype(jnp.int32)


def in_thirds(values):
    high = values.astype(jnp.bfloat16)
    rest = values - high.astype(jnp.float32)
    middle = rest.astype(jnp.bfloat16)
    low = (rest - middle.astype(jnp.float32)).astype(jnp.bfloat16)
    return jnp.concatenate([high, middle, low], axis=1)


def prepare(where, *arrays):
    outs = [
        jax.ShapeDtypeStruct((128, WIDE), jnp.float32),
        *[jax.ShapeDtypeStruct((1, SLABS), jnp.int32)] * 3,
        jax.ShapeDtypeStruct((LIST_ROWS, 128), jnp.int32),
        jax.ShapeDtypeStruct((8, 128), jnp.int32),
        jax.ShapeDtypeStruct((2 * SLOT_ROWS, 128), jnp.float32),
    ]
    return pl.pallas_call(
        prepare_kernel,
        grid_spec=pltpu.PrefetchScalarGridSpec(
            num_scalar_prefetch=1,
            grid=(1,),
            in_specs=[whole(a) for a in arrays],
            out_specs=[whole(o) for o in outs],
        ),
        out_shape=outs,
        compiler_params=pltpu.CompilerParams(vmem_limit_bytes=VMEM),
        name="distances_and_live_rows",
    )(where, *arrays)


def last_block(step, count):
    return jnp.minimum(step, jnp.maximum((count[0, 0] + STEP - 1) // STEP - 1, 0))


def bodies_of(step, count):
    return jnp.clip(count[0, 0] - step * STEP, 0, STEP)


def filter_kernel(count, order, table, centres, first_w, second_w, first_b, second_b, out, out_d):
    step = pl.program_id(0)

    def one(index, carry):
        spread = [[], [], [], []]
        for j in range(BODY):
            slab = order[0, (step * STEP + index) * BODY + j]
            lanes = pl.ds(pl.multiple_of((slab >> 7) << 7, 128), 128)
            lane = jnp.full((TILE, 128), slab & 127, jnp.int32)
            for q in range(4):
                values = table[q * TILE : (q + 1) * TILE, lanes]
                spread[q].append(jnp.take_along_axis(values, lane, axis=1, mode="promise_in_bounds"))
        x = jnp.concatenate(spread[0], axis=0) - centres[...]
        e = jnp.exp2(-(x * x))
        both = jnp.concatenate([e.astype(jnp.bfloat16), (x * e).astype(jnp.bfloat16)], axis=1)
        first = jnp.dot(both, first_w[...], preferred_element_type=jnp.float32)
        z = 1.0 + jnp.exp(first[:, 0:128] + first_b[...])
        act = jnp.log(z) - LOG_TWO
        deriv = first[:, 128:256]
        deriv = deriv - deriv * pltpu.reciprocal(z, approx=True)
        both2 = jnp.concatenate([act.astype(jnp.bfloat16), deriv.astype(jnp.bfloat16)], axis=1)
        second = jnp.dot(both2, second_w[...], preferred_element_type=jnp.float32)
        base = second[:, 0:128] + second_b[...]
        at_row = pl.ds(pl.multiple_of(index * ROWS, ROWS), ROWS)
        out[at_row, :] = (base * jnp.concatenate(spread[1], axis=0)).astype(jnp.bfloat16)
        out_d[at_row, :] = (
            second[:, 128:256] * jnp.concatenate(spread[2], axis=0)
            + base * jnp.concatenate(spread[3], axis=0)
        ).astype(jnp.bfloat16)
        return carry

    lax.fori_loop(0, bodies_of(step, count), one, 0)


def filters(count, order, table, first_w, second_w, first_b, second_b):
    centres = np.array(KAPPA * np.arange(128) / 128.0, np.float32)[None]
    arrays = [table, jnp.asarray(centres), first_w, second_w, first_b, second_b]
    wide = pl.BlockSpec((STEP * ROWS, 128), lambda s, n, *_: (last_block(s, n), 0))
    return pl.pallas_call(
        filter_kernel,
        grid_spec=pltpu.PrefetchScalarGridSpec(
            num_scalar_prefetch=2,
            grid=(STEPS,),
            in_specs=[whole(a) for a in arrays],
            out_specs=[wide, wide],
        ),
        out_shape=[jax.ShapeDtypeStruct((SLABS * TILE, 128), jnp.bfloat16)] * 2,
        compiler_params=pltpu.CompilerParams(vmem_limit_bytes=VMEM),
        name="pair_filters",
    )(count, order, *arrays)


def laid_end_to_end(pieces, held):
    row = 0
    for piece in pieces:
        held[row : row + piece.shape[0], :] = piece[...]
        row += piece.shape[0]


def gather_kernel(lists, one_side, middle, other_side, near, far, held):
    laid_end_to_end((one_side, middle, other_side), held)

    def one(index, carry):
        a = pl.multiple_of(lists[SLOT_ROWS + (index >> 1), 2 + (index & 1)], TILE)
        b = pl.multiple_of(lists[SLOT_ROWS + 9 + (index >> 1), 2 + (index & 1)], TILE)
        o = pl.multiple_of(index * TILE, TILE)
        near[pl.ds(o, TILE), :] = held[pl.ds(a, TILE), :]
        far[pl.ds(o, TILE), :] = held[pl.ds(b, TILE), :]
        return carry

    lax.fori_loop(0, 18, one, 0)


def gather_tiles(lists, pieces):
    shape = (18 * TILE, 128)
    outs = [jax.ShapeDtypeStruct(shape, jnp.float32)] * 2
    return pl.pallas_call(
        gather_kernel,
        grid_spec=pltpu.PrefetchScalarGridSpec(
            num_scalar_prefetch=1,
            grid=(1,),
            in_specs=[whole(p) for p in pieces],
            out_specs=[whole(o) for o in outs],
            scratch_shapes=[pltpu.VMEM((NINE, 128), jnp.float32)],
        ),
        out_shape=outs,
        compiler_params=pltpu.CompilerParams(vmem_limit_bytes=VMEM),
        name="tiles_to_send",
    )(lists, *pieces)


def softplus(values):
    return jnp.maximum(values, 0.0) + jnp.log(1.0 + jnp.exp(-jnp.abs(values)))


def nt_dot(a, b):
    return lax.dot_general(a, b, (((1,), (1,)), ((), ())), preferred_element_type=jnp.float32)


CHAINS = 4


def message_kernel(
    count, order, own_rows, other_rows, filt, p0, p1, p2, p3, p4, feats, cot, out_w, out_b, fin_w, fin_b,
    new, grad, near, *totals
):
    step = pl.program_id(0)

    @pl.when(step == 0)
    def _():
        laid_end_to_end((p0, p1, p2, p3, p4), near)
        for total in totals:
            total[...] = jnp.zeros_like(total)

    def one(index, carry):
        for j in range(BODY):
            at = (step * STEP + index) * BODY + j
            h = near[pl.ds(other_rows[0, at], 1), :]
            rows = pl.ds(pl.multiple_of(index * ROWS + j * TILE, TILE), TILE)
            own = pl.ds(pl.multiple_of(own_rows[0, at], TILE), TILE)
            total = totals[j % CHAINS]
            total[own, :] = total[own, :] + filt[rows, :].astype(jnp.float32) * h
        return carry

    lax.fori_loop(0, bodies_of(step, count), one, 0)

    @pl.when(step == pl.num_programs(0) - 1)
    def _():
        cast = sum(total[...] for total in totals).astype(jnp.bfloat16)
        pre = jnp.dot(cast, out_w[...], preferred_element_type=jnp.float32) + out_b[...]
        act = (softplus(pre) - LOG_TWO).astype(jnp.bfloat16)
        update = jnp.dot(act, fin_w[...], preferred_element_type=jnp.float32) + fin_b[...]
        new[...] = (feats[...].astype(jnp.float32) + update).astype(jnp.bfloat16)
        d_out = nt_dot(cot[...], fin_w[...])
        d_pre = (d_out * jax.nn.sigmoid(pre)).astype(jnp.bfloat16)
        grad[...] = nt_dot(d_pre, out_w[...])


def back_kernel(
    count, order, own_rows, other_rows, filt, filt_d, h0, h1, h2, h3, h4, g0, g1, g2, g3, g4, own_h, own_g,
    r_near, r_own, cot, in_w, grad, force, near, g_near, *totals
):
    step = pl.program_id(0)
    pushes = totals[CHAINS:]
    totals = totals[:CHAINS]

    @pl.when(step == 0)
    def _():
        laid_end_to_end((h0, h1, h2, h3, h4), near)
        laid_end_to_end((g0, g1, g2, g3, g4), g_near)
        for total in (*totals, *pushes):
            total[...] = jnp.zeros_like(total)

    def one(index, carry):
        slopes = []
        places = []
        for j in range(BODY):
            at = (step * STEP + index) * BODY + j
            slab = order[0, at]
            row = pl.ds(other_rows[0, at], 1)
            h = near[row, :]
            g = g_near[row, :]
            rows = pl.ds(pl.multiple_of(index * ROWS + j * TILE, TILE), TILE)
            own = pl.ds(pl.multiple_of(own_rows[0, at], TILE), TILE)
            total = totals[j % CHAINS]
            total[own, :] = total[own, :] + filt[rows, :].astype(jnp.float32) * g
            mixed = filt_d[rows, :].astype(jnp.float32) * (own_g[own, :] * h + own_h[own, :] * g)
            slopes.append(mixed.astype(jnp.bfloat16))
            places.append((own, slab))
        sums = jnp.dot(
            jnp.concatenate(slopes, axis=0),
            jnp.ones((128, 128), jnp.bfloat16),
            preferred_element_type=jnp.float32,
        )
        for j, (own, slab) in enumerate(places):
            push = pushes[j % CHAINS]
            away = r_near[pl.ds(slab, 1), :] - r_own[own, :]
            push[own, :] = push[own, :] + sums[j * TILE : (j + 1) * TILE, :] * away
        return carry

    lax.fori_loop(0, bodies_of(step, count), one, 0)

    @pl.when(step == pl.num_programs(0) - 1)
    def _():
        cast = sum(total[...] for total in totals).astype(jnp.bfloat16)
        grad[...] = cot[...].astype(jnp.float32) + nt_dot(cast, in_w[...])
        force[...] = sum(push[...] for push in pushes).T[0:8, :]


def pair_call(body, scalars, streams, arrays, outs, tables, scratch, name):
    stream = pl.BlockSpec((STEP * ROWS, 128), lambda s, n, *_: (last_block(s, n), 0))
    return pl.pallas_call(
        body,
        grid_spec=pltpu.PrefetchScalarGridSpec(
            num_scalar_prefetch=4,
            grid=(STEPS,),
            in_specs=[stream] * len(streams) + [whole(a) for a in arrays],
            out_specs=[whole(o) for o in outs],
            scratch_shapes=[pltpu.VMEM((AROUND_ROWS, 128), jnp.float32)] * tables
            + [pltpu.VMEM((256, 128), jnp.float32)] * scratch,
        ),
        out_shape=outs,
        compiler_params=pltpu.CompilerParams(vmem_limit_bytes=VMEM),
        name=name,
    )(*scalars, *streams, *arrays)


def swapped(to_far, to_near, axis):
    size = lax.axis_size(axis)
    near = [(i, i ^ 1) for i in range(size)]
    far = [(i, ((i ^ 1) + 2 * (2 * (i % 2) - 1)) % size) for i in range(size)]
    from_far = lax.ppermute(to_far, axis, far)
    return lax.ppermute(to_near, axis, near), from_far


def planes(own):
    near, far = swapped(own, own, "gz")
    return jnp.concatenate([near, own, far], axis=0)


def columns(three):
    near, far = swapped(three, three, "gx")
    return [near, three, far]


def block_diagonal(weight):
    zero = jnp.zeros_like(weight)
    return jnp.concatenate(
        [jnp.concatenate([weight, zero], axis=1), jnp.concatenate([zero, weight], axis=1)], axis=0
    )


def on_device(
    features,
    positions,
    counts,
    pair_tiles,
    input_weight,
    radial_weight,
    radial_bias,
    filter_weight,
    filter_bias,
    output_weight,
    output_bias,
    final_weight,
    final_bias,
    cotangent,
):
    own_features = features.reshape(256, 128)
    own_pos = positions.reshape(3, 256)
    hidden = jnp.dot(own_features, input_weight, preferred_element_type=jnp.float32)
    numbers = jnp.concatenate([counts.reshape(1), pair_tiles.reshape(56)]).astype(jnp.float32)
    meta = jnp.concatenate(
        [own_pos.reshape(6, 128), jnp.pad(numbers, (0, 71))[None], jnp.zeros((1, 128), jnp.float32)],
        axis=0,
    )
    three = planes(jnp.concatenate([hidden, meta], axis=0)[None])
    meta_three = three[:, 256:].reshape(1, 24 * 128)
    hidden_three = three[:, :256].reshape(768, 128)

    across = lax.axis_size("gy")
    along = lax.axis_size("gx")
    everyone = lax.all_to_all(
        jnp.broadcast_to(meta_three.reshape(1, 24, 128), (along * across, 24, 128)),
        ("gx", "gy"),
        0,
        0,
    ).reshape(along * across, 24 * 128)
    everyone = everyone.reshape(along * across * 3, 8 * 128)
    side = np.array(SLOTS)
    sides = np.zeros((SLOT_ROWS, 4), np.int32)
    sides[:28, :3] = side
    sides[:28, 3] = 1
    selectors = [list_selectors((-1, 1)), list_selectors((1, -1))]
    units = np.arange(WIDE)[None] // TILE == np.arange(2 * SLOT_ROWS)[:, None]
    where = jnp.stack([lax.axis_index(axis) for axis in ("gx", "gy", "gz")]).astype(jnp.int32)
    table, order, own_rows, other_rows, lists, count, at_unit = prepare(
        where,
        everyone,
        jnp.asarray(np.stack([rows for rows, _ in selectors])),
        jnp.asarray(np.stack([lanes for _, lanes in selectors])),
        jnp.asarray(list_bases()),
        jnp.asarray(sides),
        jnp.asarray(sides[:, :3].astype(np.float32)),
        own_pos.reshape(3, 8, TILE).transpose(0, 2, 1).reshape(96, 8),
        jnp.asarray(np.tile(units, (3, 1)).astype(jnp.bfloat16)),
    )
    near_x = columns(hidden_three)
    to_near, to_far, count = lax.optimization_barrier((*gather_tiles(lists, near_x), count))
    near = [*near_x, *swapped(to_far, to_near, "gy")]
    filt, filt_d = filters(
        count,
        order,
        table,
        block_diagonal(radial_weight),
        block_diagonal(filter_weight),
        radial_bias[None],
        filter_bias[None],
    )
    cot = cotangent.reshape(256, 128)
    scalars = (count, order, own_rows, other_rows)
    new_features, d_msg = pair_call(
        message_kernel,
        scalars,
        [filt],
        [
            *near,
            own_features,
            cot,
            output_weight,
            output_bias[None],
            final_weight,
            final_bias[None],
        ],
        [
            jax.ShapeDtypeStruct((256, 128), jnp.bfloat16),
            jax.ShapeDtypeStruct((256, 128), jnp.float32),
        ],
        1,
        CHAINS,
        "messages_and_update",
    )
    g_x = columns(planes(d_msg))
    to_near, to_far = gather_tiles(lists, g_x)
    g_near = [*g_x, *swapped(to_far, to_near, "gy")]
    r_near = at_unit[:, :96].reshape(2 * SLOT_ROWS, 3, TILE).transpose(0, 2, 1).reshape(WIDE, 3)
    r_near = jnp.pad(r_near, ((0, 0), (0, 125)))
    r_own = jnp.pad(own_pos.T, ((0, 0), (0, 125)))
    grad_features, force = pair_call(
        back_kernel,
        scalars,
        [filt, filt_d],
        [*near, *g_near, hidden, d_msg, r_near, r_own, cot, input_weight],
        [
            jax.ShapeDtypeStruct((256, 128), jnp.float32),
            jax.ShapeDtypeStruct((8, 256), jnp.float32),
        ],
        2,
        2 * CHAINS,
        "pair_gradients",
    )
    return (
        new_features.reshape(1, 1, 1, 256, 128),
        grad_features.reshape(1, 1, 1, 256, 128),
        force[:3].reshape(1, 1, 1, 3, 256),
    )


def solution(mesh):
    block = P("gx", "gy", "gz", None, None)
    return jax.shard_map(
        on_device,
        mesh=mesh,
        in_specs=(
            block,
            block,
            P("gx", "gy", "gz"),
            P("gx", "gy", "gz", None, None, None),
            *([P()] * 9),
            block,
        ),
        out_specs=(block, block, block),
        check_vma=False,
    )
```

```python
import math

import jax
import jax.numpy as jnp
import numpy as np
from jax import lax
from jax.experimental import pallas as pl
from jax.experimental.pallas import tpu as pltpu
from jax.sharding import PartitionSpec as P

TILE = 32
SOFTEN = 0.05
GAMMA = 40.0
LOG_TWO = math.log(2.0)
KAPPA = math.sqrt(GAMMA / LOG_TWO)
UNITS = 56
VMEM = 56 * 1024 * 1024


def half_shell():
    offsets = [(0, 0, 0), (1, 0, 0)]
    for step_x in (-1, 0, 1):
        offsets.append((step_x, 1, 0))
    for step_x in (-1, 0, 1):
        for step_y in (-1, 0, 1):
            offsets.append((step_x, step_y, 1))
    return offsets


SHELL = half_shell()
AROUND = [
    (sx, sy, sz)
    for sy in (0, 1, -1)
    for sx in (-1, 0, 1)
    for sz in (-1, 0, 1)
    if (sx, sy, sz) != (0, 0, 0)
]
SLOTS = [(0, 0, 0), (0, 0, 0)] + AROUND


def shell_place(offset):
    if offset in SHELL:
        return SHELL.index(offset), True
    return SHELL.index(tuple(-step for step in offset)), False


SLOT_ROWS = 32
LIST_ROWS = 56
SENT = [(sx, sz) for sx in (-1, 0, 1) for sz in (-1, 0, 1)]


def list_selectors(sides):
    rows = {0: (SLOTS[0], SLOTS[0], 0, True), 1: (SLOTS[0], SLOTS[0], 0, False)}
    for i, offset in enumerate(AROUND):
        rows[2 + i] = (SLOTS[0], offset, *shell_place(offset))
    for j, side in enumerate(sides):
        for m, (sx, sz) in enumerate(SENT):
            offset = (sx, side, sz)
            rows[SLOT_ROWS + 9 * j + m] = ((0, -side, 0), offset, *shell_place(offset))
    holders = np.zeros((LIST_ROWS, SLOT_ROWS), np.float32)
    lanes = np.zeros((4, LIST_ROWS, 128), np.float32)
    for i, (reader, offset, index_k, ahead) in rows.items():
        holder = reader if ahead else tuple(a + b for a, b in zip(reader, offset))
        holders[i, SLOTS.index(holder)] = 1.0
        for q in range(4):
            lanes[q, i, 1 + 4 * index_k + (q if ahead else (q + 2) % 4)] = 1.0
    return holders, lanes


def list_bases():
    def place_of(steps, odd):
        return 1 - steps * (1 - 2 * odd)

    def rows(odd_x, odd_y, odd_z):
        bases = np.zeros((LIST_ROWS, 3), np.float32)
        for i, (sx, sy, sz) in enumerate(SLOTS):
            if sy == 0:
                first = (place_of(sx, odd_x) * 3 + place_of(sz, odd_z)) * 256
                bases[i] = first, first, TILE
            else:
                listed = (sx + 1) * 3 + sz + 1
                first = NINE + 576 * place_of(sy, odd_y) // 2 + listed * 2 * TILE
                bases[i] = first, first + TILE, 0
        for i, (sx, sz) in enumerate(SENT):
            first = (place_of(sx, odd_x) * 3 + place_of(sz, odd_z)) * 256
            for at in (SLOT_ROWS + i, SLOT_ROWS + 9 + i):
                bases[at] = first, first, TILE
        return bases

    even = rows(0, 0, 0)
    return np.stack([even, rows(1, 0, 0) - even, rows(0, 1, 0) - even, rows(0, 0, 1) - even])


def whole(array):
    return pl.BlockSpec(array.shape, lambda s, *_: (0,) * array.ndim)


def exact_dot(a, b):
    return jnp.dot(a, b, precision=lax.Precision.HIGHEST)


BODY = 64
ROWS = BODY * TILE
SLABS = UNITS * TILE
NINE = 9 * 256
AROUND_ROWS = NINE + 2 * 18 * TILE
BODIES = SLABS // BODY
WIDE = 2 * SLOT_ROWS * TILE
IDLE = 28 * TILE
STEP = 2
STEPS = BODIES // STEP


def prepare_kernel(
    where, everyone, holders, lanes, bases, side, shift, own_side, units,
    table, order, own_rows, other_rows, lists, count, at_unit
):
    f32 = jnp.float32
    odd = [where[a] & 1 for a in range(3)]
    device = ((where[0] + side[:, 0:1]) & 3) * 4 + ((where[1] + side[:, 1:2]) & 3)
    device = device * 3 + 1 - side[:, 2:3] * (1 - 2 * odd[2])
    device = jnp.where(side[:, 3:4] > 0, device, -1)
    devices = lax.broadcasted_iota(jnp.int32, (SLOT_ROWS, 48), 1)
    slots = exact_dot(jnp.where(devices == device, 1.0, 0.0), everyone[...])
    numbers = slots[:, 768:896]
    rows = exact_dot(holders[odd[1]], numbers)
    tiles = [jnp.sum(rows * lanes[odd[1], q], axis=1, keepdims=True) for q in range(4)]
    lane = lax.broadcasted_iota(jnp.int32, (LIST_ROWS, 128), 1)
    base = bases[0]
    for a in range(3):
        base = base + bases[1 + a] * odd[a].astype(f32)
    place = [base[:, n : n + 1] + base[:, 2:3] * tiles[2 + n] for n in range(2)]
    listed = jnp.where(lane < 1, tiles[0], jnp.where(lane < 2, tiles[1], place[1]))
    listed = jnp.where(lane == 2, place[0], listed)
    lists[...] = jnp.round(listed.T[0:8, :]).astype(jnp.int32)

    slot = lax.broadcasted_iota(jnp.int32, (SLOT_ROWS, 1), 0)
    halves = []
    for n in range(2):
        own = tiles[n][0:SLOT_ROWS]
        other = tiles[2 + n][0:SLOT_ROWS]
        at = []
        for c in range(3):
            acc = jnp.zeros((SLOT_ROWS, TILE), f32)
            for t in range(8):
                first = c * 256 + t * TILE
                acc = acc + jnp.where(jnp.abs(other - t) < 0.5, slots[:, first : first + TILE], 0.0)
            at.append(acc + shift[:, c : c + 1])
        same = jnp.where((jnp.abs(own - other) < 0.5) & (slot < 2), 1.0, 0.0)
        own_left = numbers[0:1, 0:1] - own * TILE
        other_left = numbers[:, 0:1] - other * TILE
        rest = jnp.where(lane[0:SLOT_ROWS, 0:TILE] == 0, own, 0.0)
        for q, value in enumerate((own_left, other_left, same, place[n][0:SLOT_ROWS] * (1.0 / TILE))):
            rest = jnp.where(lane[0:SLOT_ROWS, 0:TILE] == q + 1, value, rest)
        halves.append(jnp.concatenate([*at, rest], axis=1))
    per_unit = jnp.concatenate(halves, axis=0)
    one_beside = lax.broadcasted_iota(jnp.int32, (2 * SLOT_ROWS, 128), 1) >= 96
    at_unit[...] = jnp.where(one_beside, 1.0, per_unit)
    per_slab = jnp.dot(in_thirds(per_unit.T), units[...], preferred_element_type=f32)

    slab = lax.broadcasted_iota(jnp.int32, (TILE, WIDE), 1)
    u = lax.broadcasted_iota(jnp.int32, (TILE, WIDE), 0)
    w = slab & (TILE - 1)
    own_tile = per_slab[96:97]
    eight = lax.broadcasted_iota(jnp.int32, (8, WIDE), 0).astype(f32)
    chosen = jnp.where(jnp.abs(own_tile - eight) < 0.5, 1.0, 0.0).astype(jnp.bfloat16)
    own_at = jnp.dot(
        in_thirds(own_side[...]), jnp.concatenate([chosen] * 3, axis=0), preferred_element_type=f32
    )
    square = jnp.full((TILE, WIDE), SOFTEN * SOFTEN, f32)
    for c in range(3):
        part = slice(c * TILE, (c + 1) * TILE)
        other_at = jnp.sum(jnp.where(u == w, per_slab[part], 0.0), axis=0, keepdims=True)
        sep = other_at - own_at[part]
        square = square + sep * sep
    dist = jnp.sqrt(square)
    reverse = ((slab >> 5) & (SLOT_ROWS - 1)) == 1
    away = jnp.where(reverse, u - w, w - u)
    drop = (per_slab[99:100] > 0.5) & (away <= 0)
    fits = (u.astype(f32) < per_slab[97:98]) & (w.astype(f32) < per_slab[98:99])
    usable = fits & (dist < 1.0) & jnp.logical_not(drop)
    angle = math.pi * dist
    near = 1.0 / dist
    cut = jnp.where(usable, 0.5 * (jnp.cos(angle) + 1.0), 0.0)
    table[0:TILE, :] = KAPPA * dist
    table[TILE : 2 * TILE, :] = cut
    table[2 * TILE : 3 * TILE, :] = cut * (-2.0 * GAMMA / KAPPA) * near
    table[3 * TILE : 4 * TILE, :] = jnp.where(usable, -0.5 * math.pi * jnp.sin(angle), 0.0) * near

    live = jnp.max(jnp.where(usable, 1.0, 0.0), axis=0, keepdims=True)
    blocks = WIDE // 128
    live = jnp.concatenate([live[:, b * 128 : (b + 1) * 128] for b in range(blocks)], axis=0)
    row = lax.broadcasted_iota(jnp.int32, (128, 128), 0)
    col = lax.broadcasted_iota(jnp.int32, (128, 128), 1)
    upto = jnp.where(row <= col, 1.0, 0.0).astype(jnp.bfloat16)
    until = jnp.dot(live.astype(jnp.bfloat16), upto, preferred_element_type=f32)
    sums = jnp.broadcast_to(until[:, 127:128], (blocks, 128)).astype(jnp.bfloat16)
    below = jnp.where(row > col, 1.0, 0.0).astype(jnp.bfloat16)[0:blocks, 0:blocks]
    before = jnp.dot(below, sums, preferred_element_type=f32)
    rank = jnp.where(live > 0.5, until + before - 1.0, -1.0)
    total = before[blocks - 1 : blocks, :] + until[blocks - 1 : blocks, 127:128]
    bodies = jnp.floor((total + (BODY - 1.0)) * (1.0 / BODY))
    count[...] = jnp.broadcast_to(bodies, (8, 128)).astype(jnp.int32)
    target = lax.broadcasted_iota(jnp.int32, (SLABS, 256), 0).astype(f32)
    names_row = lax.broadcasted_iota(jnp.int32, (8, 256), 0)
    names_lane = lax.broadcasted_iota(jnp.int32, (8, 256), 1)
    found = jnp.zeros((8, SLABS), f32)
    for b in range(blocks // 2):
        wide_rank = jnp.concatenate([rank[2 * b : 2 * b + 1], rank[2 * b + 1 : 2 * b + 2]], axis=1)
        hit = jnp.where(target == wide_rank, 1.0, 0.0).astype(jnp.bfloat16)
        names = jnp.where(names_row == 0, b * 8 + (names_lane >> 5), names_lane & (TILE - 1))
        names = jnp.where(names_row == 2, 1, names).astype(f32)
        part = slice(b * 256, (b + 1) * 256)
        names = jnp.where(names_row == 3, per_slab[96:97, part], names)
        names = jnp.where(names_row == 4, per_slab[100:101, part], names)
        found = found + nt_dot(names.astype(jnp.bfloat16), hit)
    named = jnp.where(found[2:3] > 0.5, found[0:1] * TILE + found[1:2], 1.0 * IDLE)
    order[...] = jnp.round(named).astype(jnp.int32)
    own_rows[...] = jnp.round(found[3:4] * TILE).astype(jnp.int32)
    other_rows[...] = jnp.round(found[4:5] * TILE + found[1:2]).astype(jnp.int32)


def in_thirds(values):
    high = values.astype(jnp.bfloat16)
    rest = values - high.astype(jnp.float32)
    middle = rest.astype(jnp.bfloat16)
    low = (rest - middle.astype(jnp.float32)).astype(jnp.bfloat16)
    return jnp.concatenate([high, middle, low], axis=1)


def prepare(where, *arrays):
    outs = [
        jax.ShapeDtypeStruct((128, WIDE), jnp.float32),
        *[jax.ShapeDtypeStruct((1, SLABS), jnp.int32)] * 3,
        jax.ShapeDtypeStruct((8, LIST_ROWS), jnp.int32),
        jax.ShapeDtypeStruct((8, 128), jnp.int32),
        jax.ShapeDtypeStruct((2 * SLOT_ROWS, 128), jnp.float32),
    ]
    return pl.pallas_call(
        prepare_kernel,
        grid_spec=pltpu.PrefetchScalarGridSpec(
            num_scalar_prefetch=1,
            grid=(1,),
            in_specs=[whole(a) for a in arrays],
            out_specs=[whole(o) for o in outs],
        ),
        out_shape=outs,
        compiler_params=pltpu.CompilerParams(vmem_limit_bytes=VMEM),
        name="distances_and_live_rows",
    )(where, *arrays)


def last_block(step, count):
    return jnp.minimum(step, jnp.maximum((count[0, 0] + STEP - 1) // STEP - 1, 0))


def bodies_of(step, count):
    return jnp.clip(count[0, 0] - step * STEP, 0, STEP)


def filter_kernel(
    count, order, table, centres, first_128, second_128, first_b, second_b, out, out_d, first_w, second_w
):
    step = pl.program_id(0)

    @pl.when(step == 0)
    def _():
        for wide_w, weight in ((first_w, first_128), (second_w, second_128)):
            wide_w[...] = jnp.zeros_like(wide_w)
            wide_w[0:128, 0:128] = weight[...]
            wide_w[128:256, 128:256] = weight[...]


    def one(index, carry):
        spread = [[], [], [], []]
        for j in range(BODY):
            slab = order[0, (step * STEP + index) * BODY + j]
            lanes = pl.ds(pl.multiple_of((slab >> 7) << 7, 128), 128)
            lane = jnp.full((TILE, 128), slab & 127, jnp.int32)
            for q in range(4):
                values = table[q * TILE : (q + 1) * TILE, lanes]
                spread[q].append(jnp.take_along_axis(values, lane, axis=1, mode="promise_in_bounds"))
        x = jnp.concatenate(spread[0], axis=0) - centres[...]
        e = jnp.exp2(-(x * x))
        both = jnp.concatenate([e.astype(jnp.bfloat16), (x * e).astype(jnp.bfloat16)], axis=1)
        first = jnp.dot(both, first_w[...], preferred_element_type=jnp.float32)
        z = 1.0 + jnp.exp(first[:, 0:128] + first_b[...])
        act = jnp.log(z) - LOG_TWO
        deriv = first[:, 128:256]
        deriv = deriv - deriv * pltpu.reciprocal(z, approx=True)
        both2 = jnp.concatenate([act.astype(jnp.bfloat16), deriv.astype(jnp.bfloat16)], axis=1)
        second = jnp.dot(both2, second_w[...], preferred_element_type=jnp.float32)
        base = second[:, 0:128] + second_b[...]
        at_row = pl.ds(pl.multiple_of(index * ROWS, ROWS), ROWS)
        out[at_row, :] = (base * jnp.concatenate(spread[1], axis=0)).astype(jnp.bfloat16)
        out_d[at_row, :] = (
            second[:, 128:256] * jnp.concatenate(spread[2], axis=0)
            + base * jnp.concatenate(spread[3], axis=0)
        ).astype(jnp.bfloat16)
        return carry

    lax.fori_loop(0, bodies_of(step, count), one, 0)


def filters(count, order, table, first_w, second_w, first_b, second_b):
    centres = np.array(KAPPA * np.arange(128) / 128.0, np.float32)[None]
    arrays = [table, jnp.asarray(centres), first_w, second_w, first_b, second_b]
    wide = pl.BlockSpec((STEP * ROWS, 128), lambda s, n, *_: (last_block(s, n), 0))
    return pl.pallas_call(
        filter_kernel,
        grid_spec=pltpu.PrefetchScalarGridSpec(
            num_scalar_prefetch=2,
            grid=(STEPS,),
            in_specs=[whole(a) for a in arrays],
            out_specs=[wide, wide],
            scratch_shapes=[pltpu.VMEM((256, 256), jnp.bfloat16)] * 2,
        ),
        out_shape=[jax.ShapeDtypeStruct((SLABS * TILE, 128), jnp.bfloat16)] * 2,
        compiler_params=pltpu.CompilerParams(vmem_limit_bytes=VMEM),
        name="pair_filters",
    )(count, order, *arrays)


def laid_end_to_end(pieces, held):
    row = 0
    for piece in pieces:
        held[row : row + piece.shape[0], :] = piece[...]
        row += piece.shape[0]


def gather_kernel(lists, one_side, middle, other_side, near, far, held):
    laid_end_to_end((one_side, middle, other_side), held)

    def one(index, carry):
        a = pl.multiple_of(lists[2 + (index & 1), SLOT_ROWS + (index >> 1)], TILE)
        b = pl.multiple_of(lists[2 + (index & 1), SLOT_ROWS + 9 + (index >> 1)], TILE)
        o = pl.multiple_of(index * TILE, TILE)
        near[pl.ds(o, TILE), :] = held[pl.ds(a, TILE), :]
        far[pl.ds(o, TILE), :] = held[pl.ds(b, TILE), :]
        return carry

    lax.fori_loop(0, 18, one, 0)


def gather_tiles(lists, pieces):
    shape = (18 * TILE, 128)
    outs = [jax.ShapeDtypeStruct(shape, jnp.float32)] * 2
    return pl.pallas_call(
        gather_kernel,
        grid_spec=pltpu.PrefetchScalarGridSpec(
            num_scalar_prefetch=1,
            grid=(1,),
            in_specs=[whole(p) for p in pieces],
            out_specs=[whole(o) for o in outs],
            scratch_shapes=[pltpu.VMEM((NINE, 128), jnp.float32)],
        ),
        out_shape=outs,
        compiler_params=pltpu.CompilerParams(vmem_limit_bytes=VMEM),
        name="tiles_to_send",
    )(lists, *pieces)


def softplus(values):
    return jnp.maximum(values, 0.0) + jnp.log(1.0 + jnp.exp(-jnp.abs(values)))


def nt_dot(a, b):
    return lax.dot_general(a, b, (((1,), (1,)), ((), ())), preferred_element_type=jnp.float32)


CHAINS = 4


def message_kernel(
    count, order, own_rows, other_rows, filt, p0, p1, p2, p3, p4, feats, cot, out_w, out_b, fin_w, fin_b,
    new, grad, near, *totals
):
    step = pl.program_id(0)

    @pl.when(step == 0)
    def _():
        laid_end_to_end((p0, p1, p2, p3, p4), near)
        for total in totals:
            total[...] = jnp.zeros_like(total)

    def one(index, carry):
        for j in range(BODY):
            at = (step * STEP + index) * BODY + j
            h = near[pl.ds(other_rows[0, at], 1), :]
            rows = pl.ds(pl.multiple_of(index * ROWS + j * TILE, TILE), TILE)
            own = pl.ds(pl.multiple_of(own_rows[0, at], TILE), TILE)
            total = totals[j % CHAINS]
            total[own, :] = total[own, :] + filt[rows, :].astype(jnp.float32) * h
        return carry

    lax.fori_loop(0, bodies_of(step, count), one, 0)

    @pl.when(step == pl.num_programs(0) - 1)
    def _():
        cast = sum(total[...] for total in totals).astype(jnp.bfloat16)
        pre = jnp.dot(cast, out_w[...], preferred_element_type=jnp.float32) + out_b[...]
        act = (softplus(pre) - LOG_TWO).astype(jnp.bfloat16)
        update = jnp.dot(act, fin_w[...], preferred_element_type=jnp.float32) + fin_b[...]
        new[...] = (feats[...].astype(jnp.float32) + update).astype(jnp.bfloat16)
        d_out = nt_dot(cot[...], fin_w[...])
        d_pre = (d_out * jax.nn.sigmoid(pre)).astype(jnp.bfloat16)
        grad[...] = nt_dot(d_pre, out_w[...])


def back_kernel(
    count, order, own_rows, other_rows, filt, filt_d, h0, h1, h2, h3, h4, g0, g1, g2, g3, g4, own_h, own_g,
    r_near, r_own, cot, in_w, grad, force, near, g_near, *totals
):
    step = pl.program_id(0)
    pushes = totals[CHAINS:]
    totals = totals[:CHAINS]

    @pl.when(step == 0)
    def _():
        laid_end_to_end((h0, h1, h2, h3, h4), near)
        laid_end_to_end((g0, g1, g2, g3, g4), g_near)
        for total in (*totals, *pushes):
            total[...] = jnp.zeros_like(total)

    def one(index, carry):
        slopes = []
        places = []
        for j in range(BODY):
            at = (step * STEP + index) * BODY + j
            slab = order[0, at]
            row = pl.ds(other_rows[0, at], 1)
            h = near[row, :]
            g = g_near[row, :]
            rows = pl.ds(pl.multiple_of(index * ROWS + j * TILE, TILE), TILE)
            own = pl.ds(pl.multiple_of(own_rows[0, at], TILE), TILE)
            total = totals[j % CHAINS]
            total[own, :] = total[own, :] + filt[rows, :].astype(jnp.float32) * g
            mixed = filt_d[rows, :].astype(jnp.float32) * (own_g[own, :] * h + own_h[own, :] * g)
            slopes.append(mixed.astype(jnp.bfloat16))
            places.append((own, slab))
        sums = jnp.dot(
            jnp.concatenate(slopes, axis=0),
            jnp.ones((128, 128), jnp.bfloat16),
            preferred_element_type=jnp.float32,
        )
        for j, (own, slab) in enumerate(places):
            push = pushes[j % CHAINS]
            push[own, :] = push[own, :] + sums[j * TILE : (j + 1) * TILE, :] * r_near[pl.ds(slab, 1), :]
        return carry

    lax.fori_loop(0, bodies_of(step, count), one, 0)

    @pl.when(step == pl.num_programs(0) - 1)
    def _():
        cast = sum(total[...] for total in totals).astype(jnp.bfloat16)
        grad[...] = cot[...].astype(jnp.float32) + nt_dot(cast, in_w[...])
        moments = sum(push[...] for push in pushes).T
        force[...] = moments[0:3, :] - r_own[...] * moments[3:4, :]


def pair_call(body, scalars, streams, arrays, outs, tables, scratch, name):
    stream = pl.BlockSpec((STEP * ROWS, 128), lambda s, n, *_: (last_block(s, n), 0))
    return pl.pallas_call(
        body,
        grid_spec=pltpu.PrefetchScalarGridSpec(
            num_scalar_prefetch=4,
            grid=(STEPS,),
            in_specs=[stream] * len(streams) + [whole(a) for a in arrays],
            out_specs=[whole(o) for o in outs],
            scratch_shapes=[pltpu.VMEM((AROUND_ROWS, 128), jnp.float32)] * tables
            + [pltpu.VMEM((256, 128), jnp.float32)] * scratch,
        ),
        out_shape=outs,
        compiler_params=pltpu.CompilerParams(vmem_limit_bytes=VMEM),
        name=name,
    )(*scalars, *streams, *arrays)


def swapped(to_far, to_near, axis):
    size = lax.axis_size(axis)
    near = [(i, i ^ 1) for i in range(size)]
    far = [(i, ((i ^ 1) + 2 * (2 * (i % 2) - 1)) % size) for i in range(size)]
    from_far = lax.ppermute(to_far, axis, far)
    return lax.ppermute(to_near, axis, near), from_far


def planes(own):
    near, far = swapped(own, own, "gz")
    return jnp.concatenate([near, own, far], axis=0)


def columns(three):
    near, far = swapped(three, three, "gx")
    return [near, three, far]


def on_device(
    features,
    positions,
    counts,
    pair_tiles,
    input_weight,
    radial_weight,
    radial_bias,
    filter_weight,
    filter_bias,
    output_weight,
    output_bias,
    final_weight,
    final_bias,
    cotangent,
):
    own_features = features.reshape(256, 128)
    own_pos = positions.reshape(3, 256)
    hidden = jnp.dot(own_features, input_weight, preferred_element_type=jnp.float32)
    numbers = jnp.concatenate([counts.reshape(1), pair_tiles.reshape(56)]).astype(jnp.float32)
    meta = jnp.concatenate(
        [own_pos.reshape(6, 128), jnp.pad(numbers, (0, 71))[None], jnp.zeros((1, 128), jnp.float32)],
        axis=0,
    )
    three = planes(jnp.concatenate([hidden, meta], axis=0)[None])
    meta_three = three[:, 256:].reshape(1, 24 * 128)
    hidden_three = three[:, :256].reshape(768, 128)

    across = lax.axis_size("gy")
    along = lax.axis_size("gx")
    everyone = lax.all_to_all(
        jnp.broadcast_to(meta_three.reshape(1, 24, 128), (along * across, 24, 128)),
        ("gx", "gy"),
        0,
        0,
    ).reshape(along * across, 24 * 128)
    everyone = everyone.reshape(along * across * 3, 8 * 128)
    side = np.array(SLOTS)
    sides = np.zeros((SLOT_ROWS, 4), np.int32)
    sides[:28, :3] = side
    sides[:28, 3] = 1
    selectors = [list_selectors((-1, 1)), list_selectors((1, -1))]
    units = np.arange(WIDE)[None] // TILE == np.arange(2 * SLOT_ROWS)[:, None]
    where = jnp.stack([lax.axis_index(axis) for axis in ("gx", "gy", "gz")]).astype(jnp.int32)
    table, order, own_rows, other_rows, lists, count, at_unit = prepare(
        where,
        everyone,
        jnp.asarray(np.stack([rows for rows, _ in selectors])),
        jnp.asarray(np.stack([lanes for _, lanes in selectors])),
        jnp.asarray(list_bases()),
        jnp.asarray(sides),
        jnp.asarray(sides[:, :3].astype(np.float32)),
        own_pos.reshape(3, 8, TILE).transpose(0, 2, 1).reshape(96, 8),
        jnp.asarray(np.tile(units, (3, 1)).astype(jnp.bfloat16)),
    )
    near_x = columns(hidden_three)
    to_near, to_far, count = lax.optimization_barrier((*gather_tiles(lists, near_x), count))
    near = [*near_x, *swapped(to_far, to_near, "gy")]
    filt, filt_d = filters(
        count,
        order,
        table,
        radial_weight,
        filter_weight,
        radial_bias[None],
        filter_bias[None],
    )
    cot = cotangent.reshape(256, 128)
    scalars = (count, order, own_rows, other_rows)
    new_features, d_msg = pair_call(
        message_kernel,
        scalars,
        [filt],
        [
            *near,
            own_features,
            cot,
            output_weight,
            output_bias[None],
            final_weight,
            final_bias[None],
        ],
        [
            jax.ShapeDtypeStruct((256, 128), jnp.bfloat16),
            jax.ShapeDtypeStruct((256, 128), jnp.float32),
        ],
        1,
        CHAINS,
        "messages_and_update",
    )
    g_x = columns(planes(d_msg))
    to_near, to_far = gather_tiles(lists, g_x)
    g_near = [*g_x, *swapped(to_far, to_near, "gy")]
    r_near = at_unit.reshape(2 * SLOT_ROWS, 4, TILE).transpose(0, 2, 1).reshape(WIDE, 4)
    r_near = jnp.pad(r_near, ((0, 0), (0, 124)))
    grad_features, force = pair_call(
        back_kernel,
        scalars,
        [filt, filt_d],
        [*near, *g_near, hidden, d_msg, r_near, own_pos, cot, input_weight],
        [
            jax.ShapeDtypeStruct((256, 128), jnp.float32),
            jax.ShapeDtypeStruct((3, 256), jnp.float32),
        ],
        2,
        2 * CHAINS,
        "pair_gradients",
    )
    return (
        new_features.reshape(1, 1, 1, 256, 128),
        grad_features.reshape(1, 1, 1, 256, 128),
        force.reshape(1, 1, 1, 3, 256),
    )


def solution(mesh):
    block = P("gx", "gy", "gz", None, None)
    return jax.shard_map(
        on_device,
        mesh=mesh,
        in_specs=(
            block,
            block,
            P("gx", "gy", "gz"),
            P("gx", "gy", "gz", None, None, None),
            *([P()] * 9),
            block,
        ),
        out_specs=(block, block, block),
        check_vma=False,
    )
```

```python
import math

import jax
import jax.numpy as jnp
import numpy as np
from jax import lax
from jax.experimental import pallas as pl
from jax.experimental.pallas import tpu as pltpu
from jax.sharding import PartitionSpec as P

TILE = 32
SOFTEN = 0.05
GAMMA = 40.0
LOG_TWO = math.log(2.0)
KAPPA = math.sqrt(GAMMA / LOG_TWO)
UNITS = 56
VMEM = 56 * 1024 * 1024


def half_shell():
    offsets = [(0, 0, 0), (1, 0, 0)]
    for step_x in (-1, 0, 1):
        offsets.append((step_x, 1, 0))
    for step_x in (-1, 0, 1):
        for step_y in (-1, 0, 1):
            offsets.append((step_x, step_y, 1))
    return offsets


SHELL = half_shell()
AROUND = [
    (sx, sy, sz)
    for sy in (0, 1, -1)
    for sx in (-1, 0, 1)
    for sz in (-1, 0, 1)
    if (sx, sy, sz) != (0, 0, 0)
]
SLOTS = [(0, 0, 0), (0, 0, 0)] + AROUND


def shell_place(offset):
    if offset in SHELL:
        return SHELL.index(offset), True
    return SHELL.index(tuple(-step for step in offset)), False


SLOT_ROWS = 32
LIST_ROWS = 56
SENT = [(sx, sz) for sx in (-1, 0, 1) for sz in (-1, 0, 1)]


def list_selectors(sides):
    rows = {0: (SLOTS[0], SLOTS[0], 0, True), 1: (SLOTS[0], SLOTS[0], 0, False)}
    for i, offset in enumerate(AROUND):
        rows[2 + i] = (SLOTS[0], offset, *shell_place(offset))
    for j, side in enumerate(sides):
        for m, (sx, sz) in enumerate(SENT):
            offset = (sx, side, sz)
            rows[SLOT_ROWS + 9 * j + m] = ((0, -side, 0), offset, *shell_place(offset))
    holders = np.zeros((LIST_ROWS, SLOT_ROWS), np.float32)
    lanes = np.zeros((4, LIST_ROWS, 128), np.float32)
    for i, (reader, offset, index_k, ahead) in rows.items():
        holder = reader if ahead else tuple(a + b for a, b in zip(reader, offset))
        holders[i, SLOTS.index(holder)] = 1.0
        for q in range(4):
            lanes[q, i, 1 + 4 * index_k + (q if ahead else (q + 2) % 4)] = 1.0
    return holders, lanes


def list_bases():
    def place_of(steps, odd):
        return 1 - steps * (1 - 2 * odd)

    def rows(odd_x, odd_y, odd_z):
        bases = np.zeros((LIST_ROWS, 3), np.float32)
        for i, (sx, sy, sz) in enumerate(SLOTS):
            if sy == 0:
                first = (place_of(sx, odd_x) * 3 + place_of(sz, odd_z)) * 256
                bases[i] = first, first, TILE
            else:
                listed = (sx + 1) * 3 + sz + 1
                first = NINE + 576 * place_of(sy, odd_y) // 2 + listed * 2 * TILE
                bases[i] = first, first + TILE, 0
        for i, (sx, sz) in enumerate(SENT):
            first = (place_of(sx, odd_x) * 3 + place_of(sz, odd_z)) * 256
            for at in (SLOT_ROWS + i, SLOT_ROWS + 9 + i):
                bases[at] = first, first, TILE
        return bases

    even = rows(0, 0, 0)
    return np.stack([even, rows(1, 0, 0) - even, rows(0, 1, 0) - even, rows(0, 0, 1) - even])


def whole(array):
    return pl.BlockSpec(array.shape, lambda s, *_: (0,) * array.ndim)


def exact_dot(a, b):
    return jnp.dot(a, b, precision=lax.Precision.HIGHEST)


BODY = 64
ROWS = BODY * TILE
SLABS = UNITS * TILE
NINE = 9 * 256
AROUND_ROWS = NINE + 2 * 18 * TILE
BODIES = SLABS // BODY
WIDE = 2 * SLOT_ROWS * TILE
IDLE = 28 * TILE
STEP = 2
STEPS = BODIES // STEP


def prepare_kernel(
    where, everyone, holders, lanes, bases, side, shift, own_side,
    table, order, own_rows, other_rows, lists, count, at_unit
):
    f32 = jnp.float32
    odd = [where[a] & 1 for a in range(3)]
    device = ((where[0] + side[:, 0:1]) & 3) * 4 + ((where[1] + side[:, 1:2]) & 3)
    device = device * 3 + 1 - side[:, 2:3] * (1 - 2 * odd[2])
    device = jnp.where(side[:, 3:4] > 0, device, -1)
    devices = lax.broadcasted_iota(jnp.int32, (SLOT_ROWS, 48), 1)
    slots = exact_dot(jnp.where(devices == device, 1.0, 0.0), everyone[...])
    numbers = slots[:, 768:896]
    rows = exact_dot(holders[odd[1]], numbers)
    tiles = [jnp.sum(rows * lanes[odd[1], q], axis=1, keepdims=True) for q in range(4)]
    lane = lax.broadcasted_iota(jnp.int32, (LIST_ROWS, 128), 1)
    base = bases[0]
    for a in range(3):
        base = base + bases[1 + a] * odd[a].astype(f32)
    place = [base[:, n : n + 1] + base[:, 2:3] * tiles[2 + n] for n in range(2)]
    listed = jnp.where(lane < 1, tiles[0], jnp.where(lane < 2, tiles[1], place[1]))
    listed = jnp.where(lane == 2, place[0], listed)
    lists[...] = jnp.round(listed.T[0:8, :]).astype(jnp.int32)

    slot = lax.broadcasted_iota(jnp.int32, (SLOT_ROWS, 1), 0)
    halves = []
    for n in range(2):
        own = tiles[n][0:SLOT_ROWS]
        other = tiles[2 + n][0:SLOT_ROWS]
        at = []
        for c in range(3):
            acc = jnp.zeros((SLOT_ROWS, TILE), f32)
            for t in range(8):
                first = c * 256 + t * TILE
                acc = acc + jnp.where(jnp.abs(other - t) < 0.5, slots[:, first : first + TILE], 0.0)
            at.append(acc + shift[:, c : c + 1])
        same = jnp.where((jnp.abs(own - other) < 0.5) & (slot < 2), 1.0, 0.0)
        own_left = numbers[0:1, 0:1] - own * TILE
        other_left = numbers[:, 0:1] - other * TILE
        rest = jnp.where(lane[0:SLOT_ROWS, 0:TILE] == 0, own, 0.0)
        for q, value in enumerate((own_left, other_left, same, place[n][0:SLOT_ROWS] * (1.0 / TILE))):
            rest = jnp.where(lane[0:SLOT_ROWS, 0:TILE] == q + 1, value, rest)
        halves.append(jnp.concatenate([*at, rest], axis=1))
    per_unit = jnp.concatenate(halves, axis=0)
    one_beside = lax.broadcasted_iota(jnp.int32, (2 * SLOT_ROWS, 128), 1) >= 96
    at_unit[...] = jnp.where(one_beside, 1.0, per_unit)
    unit = lax.broadcasted_iota(jnp.int32, (2 * SLOT_ROWS, WIDE), 0)
    slab = lax.broadcasted_iota(jnp.int32, (2 * SLOT_ROWS, WIDE), 1)
    units = jnp.where(unit == (slab >> 5), 1.0, 0.0).astype(jnp.bfloat16)
    per_slab = jnp.dot(
        in_thirds(per_unit.T), jnp.concatenate([units] * 3, axis=0), preferred_element_type=f32
    )

    slab = lax.broadcasted_iota(jnp.int32, (TILE, WIDE), 1)
    u = lax.broadcasted_iota(jnp.int32, (TILE, WIDE), 0)
    w = slab & (TILE - 1)
    own_tile = per_slab[96:97]
    eight = lax.broadcasted_iota(jnp.int32, (8, WIDE), 0).astype(f32)
    chosen = jnp.where(jnp.abs(own_tile - eight) < 0.5, 1.0, 0.0).astype(jnp.bfloat16)
    own_at = jnp.dot(
        in_thirds(own_side[...]), jnp.concatenate([chosen] * 3, axis=0), preferred_element_type=f32
    )
    square = jnp.full((TILE, WIDE), SOFTEN * SOFTEN, f32)
    for c in range(3):
        part = slice(c * TILE, (c + 1) * TILE)
        other_at = jnp.sum(jnp.where(u == w, per_slab[part], 0.0), axis=0, keepdims=True)
        sep = other_at - own_at[part]
        square = square + sep * sep
    dist = jnp.sqrt(square)
    reverse = ((slab >> 5) & (SLOT_ROWS - 1)) == 1
    away = jnp.where(reverse, u - w, w - u)
    drop = (per_slab[99:100] > 0.5) & (away <= 0)
    fits = (u.astype(f32) < per_slab[97:98]) & (w.astype(f32) < per_slab[98:99])
    usable = fits & (dist < 1.0) & jnp.logical_not(drop)
    angle = math.pi * dist
    near = 1.0 / dist
    cut = jnp.where(usable, 0.5 * (jnp.cos(angle) + 1.0), 0.0)
    table[0:TILE, :] = KAPPA * dist
    table[TILE : 2 * TILE, :] = cut
    table[2 * TILE : 3 * TILE, :] = cut * (-2.0 * GAMMA / KAPPA) * near
    table[3 * TILE : 4 * TILE, :] = jnp.where(usable, -0.5 * math.pi * jnp.sin(angle), 0.0) * near

    live = jnp.max(jnp.where(usable, 1.0, 0.0), axis=0, keepdims=True)
    blocks = WIDE // 128
    live = jnp.concatenate([live[:, b * 128 : (b + 1) * 128] for b in range(blocks)], axis=0)
    row = lax.broadcasted_iota(jnp.int32, (128, 128), 0)
    col = lax.broadcasted_iota(jnp.int32, (128, 128), 1)
    upto = jnp.where(row <= col, 1.0, 0.0).astype(jnp.bfloat16)
    until = jnp.dot(live.astype(jnp.bfloat16), upto, preferred_element_type=f32)
    sums = jnp.broadcast_to(until[:, 127:128], (blocks, 128)).astype(jnp.bfloat16)
    below = jnp.where(row > col, 1.0, 0.0).astype(jnp.bfloat16)[0:blocks, 0:blocks]
    before = jnp.dot(below, sums, preferred_element_type=f32)
    rank = jnp.where(live > 0.5, until + before - 1.0, -1.0)
    total = before[blocks - 1 : blocks, :] + until[blocks - 1 : blocks, 127:128]
    bodies = jnp.floor((total + (BODY - 1.0)) * (1.0 / BODY))
    count[...] = jnp.broadcast_to(bodies, (8, 128)).astype(jnp.int32)
    target = lax.broadcasted_iota(jnp.int32, (256, 256), 0).astype(f32)
    names_row = lax.broadcasted_iota(jnp.int32, (8, 256), 0)
    names_lane = lax.broadcasted_iota(jnp.int32, (8, 256), 1)
    found = [jnp.zeros((8, 256), f32)] * (SLABS // 256)
    for b in range(blocks // 2):
        wide_rank = jnp.concatenate([rank[2 * b : 2 * b + 1], rank[2 * b + 1 : 2 * b + 2]], axis=1)
        names = jnp.where(names_row == 0, b * 8 + (names_lane >> 5), names_lane & (TILE - 1))
        names = jnp.where(names_row == 2, 1, names).astype(f32)
        part = slice(b * 256, (b + 1) * 256)
        names = jnp.where(names_row == 3, per_slab[96:97, part], names)
        names = jnp.where(names_row == 4, per_slab[100:101, part], names)
        names = names.astype(jnp.bfloat16)
        for i in range(min(b + 1, len(found))):
            hit = jnp.where(target == wide_rank - i * 256.0, 1.0, 0.0).astype(jnp.bfloat16)
            found[i] = found[i] + nt_dot(names, hit)
    found = jnp.concatenate(found, axis=1)
    named = jnp.where(found[2:3] > 0.5, found[0:1] * TILE + found[1:2], 1.0 * IDLE)
    order[...] = jnp.round(named).astype(jnp.int32)
    own_rows[...] = jnp.round(found[3:4] * TILE).astype(jnp.int32)
    other_rows[...] = jnp.round(found[4:5] * TILE + found[1:2]).astype(jnp.int32)


def in_thirds(values):
    high = values.astype(jnp.bfloat16)
    rest = values - high.astype(jnp.float32)
    middle = rest.astype(jnp.bfloat16)
    low = (rest - middle.astype(jnp.float32)).astype(jnp.bfloat16)
    return jnp.concatenate([high, middle, low], axis=1)


def prepare(where, *arrays):
    outs = [
        jax.ShapeDtypeStruct((128, WIDE), jnp.float32),
        *[jax.ShapeDtypeStruct((1, SLABS), jnp.int32)] * 3,
        jax.ShapeDtypeStruct((8, LIST_ROWS), jnp.int32),
        jax.ShapeDtypeStruct((8, 128), jnp.int32),
        jax.ShapeDtypeStruct((2 * SLOT_ROWS, 128), jnp.float32),
    ]
    return pl.pallas_call(
        prepare_kernel,
        grid_spec=pltpu.PrefetchScalarGridSpec(
            num_scalar_prefetch=1,
            grid=(1,),
            in_specs=[whole(a) for a in arrays],
            out_specs=[whole(o) for o in outs],
        ),
        out_shape=outs,
        compiler_params=pltpu.CompilerParams(vmem_limit_bytes=VMEM),
        name="distances_and_live_rows",
    )(where, *arrays)


def last_block(step, count):
    return jnp.minimum(step, jnp.maximum((count[0, 0] + STEP - 1) // STEP - 1, 0))


def bodies_of(step, count):
    return jnp.clip(count[0, 0] - step * STEP, 0, STEP)


def filter_kernel(
    count, order, table, centres, first_128, second_128, first_b, second_b, out, out_d, first_w, second_w
):
    step = pl.program_id(0)

    @pl.when(step == 0)
    def _():
        for wide_w, weight in ((first_w, first_128), (second_w, second_128)):
            wide_w[...] = jnp.zeros_like(wide_w)
            wide_w[0:128, 0:128] = weight[...]
            wide_w[128:256, 128:256] = weight[...]


    def one(index, carry):
        spread = [[], [], [], []]
        for j in range(BODY):
            slab = order[0, (step * STEP + index) * BODY + j]
            lanes = pl.ds(pl.multiple_of((slab >> 7) << 7, 128), 128)
            lane = jnp.full((TILE, 128), slab & 127, jnp.int32)
            for q in range(4):
                values = table[q * TILE : (q + 1) * TILE, lanes]
                spread[q].append(jnp.take_along_axis(values, lane, axis=1, mode="promise_in_bounds"))
        x = jnp.concatenate(spread[0], axis=0) - centres[...]
        e = jnp.exp2(-(x * x))
        both = jnp.concatenate([e.astype(jnp.bfloat16), (x * e).astype(jnp.bfloat16)], axis=1)
        first = jnp.dot(both, first_w[...], preferred_element_type=jnp.float32)
        z = 1.0 + jnp.exp(first[:, 0:128] + first_b[...])
        act = jnp.log(z) - LOG_TWO
        deriv = first[:, 128:256]
        deriv = deriv - deriv * pltpu.reciprocal(z, approx=True)
        both2 = jnp.concatenate([act.astype(jnp.bfloat16), deriv.astype(jnp.bfloat16)], axis=1)
        second = jnp.dot(both2, second_w[...], preferred_element_type=jnp.float32)
        base = second[:, 0:128] + second_b[...]
        at_row = pl.ds(pl.multiple_of(index * ROWS, ROWS), ROWS)
        out[at_row, :] = (base * jnp.concatenate(spread[1], axis=0)).astype(jnp.bfloat16)
        out_d[at_row, :] = (
            second[:, 128:256] * jnp.concatenate(spread[2], axis=0)
            + base * jnp.concatenate(spread[3], axis=0)
        ).astype(jnp.bfloat16)
        return carry

    lax.fori_loop(0, bodies_of(step, count), one, 0)


def filters(count, order, table, first_w, second_w, first_b, second_b):
    centres = np.array(KAPPA * np.arange(128) / 128.0, np.float32)[None]
    arrays = [table, jnp.asarray(centres), first_w, second_w, first_b, second_b]
    wide = pl.BlockSpec((STEP * ROWS, 128), lambda s, n, *_: (last_block(s, n), 0))
    return pl.pallas_call(
        filter_kernel,
        grid_spec=pltpu.PrefetchScalarGridSpec(
            num_scalar_prefetch=2,
            grid=(STEPS,),
            in_specs=[whole(a) for a in arrays],
            out_specs=[wide, wide],
            scratch_shapes=[pltpu.VMEM((256, 256), jnp.bfloat16)] * 2,
        ),
        out_shape=[jax.ShapeDtypeStruct((SLABS * TILE, 128), jnp.bfloat16)] * 2,
        compiler_params=pltpu.CompilerParams(vmem_limit_bytes=VMEM),
        name="pair_filters",
    )(count, order, *arrays)


def laid_end_to_end(pieces, held):
    row = 0
    for piece in pieces:
        held[row : row + piece.shape[0], :] = piece[...]
        row += piece.shape[0]


def gather_kernel(lists, one_side, middle, other_side, near, far, held):
    laid_end_to_end((one_side, middle, other_side), held)

    def one(index, carry):
        a = pl.multiple_of(lists[2 + (index & 1), SLOT_ROWS + (index >> 1)], TILE)
        b = pl.multiple_of(lists[2 + (index & 1), SLOT_ROWS + 9 + (index >> 1)], TILE)
        o = pl.multiple_of(index * TILE, TILE)
        near[pl.ds(o, TILE), :] = held[pl.ds(a, TILE), :]
        far[pl.ds(o, TILE), :] = held[pl.ds(b, TILE), :]
        return carry

    lax.fori_loop(0, 18, one, 0)


def gather_tiles(lists, pieces):
    shape = (18 * TILE, 128)
    outs = [jax.ShapeDtypeStruct(shape, jnp.float32)] * 2
    return pl.pallas_call(
        gather_kernel,
        grid_spec=pltpu.PrefetchScalarGridSpec(
            num_scalar_prefetch=1,
            grid=(1,),
            in_specs=[whole(p) for p in pieces],
            out_specs=[whole(o) for o in outs],
            scratch_shapes=[pltpu.VMEM((NINE, 128), jnp.float32)],
        ),
        out_shape=outs,
        compiler_params=pltpu.CompilerParams(vmem_limit_bytes=VMEM),
        name="tiles_to_send",
    )(lists, *pieces)


def softplus(values):
    return jnp.maximum(values, 0.0) + jnp.log(1.0 + jnp.exp(-jnp.abs(values)))


def nt_dot(a, b):
    return lax.dot_general(a, b, (((1,), (1,)), ((), ())), preferred_element_type=jnp.float32)


CHAINS = 4


def message_kernel(
    count, order, own_rows, other_rows, filt, p0, p1, p2, p3, p4, feats, cot, out_w, out_b, fin_w, fin_b,
    new, grad, near, *totals
):
    step = pl.program_id(0)

    @pl.when(step == 0)
    def _():
        laid_end_to_end((p0, p1, p2, p3, p4), near)
        for total in totals:
            total[...] = jnp.zeros_like(total)

    def one(index, carry):
        for j in range(BODY):
            at = (step * STEP + index) * BODY + j
            h = near[pl.ds(other_rows[0, at], 1), :]
            rows = pl.ds(pl.multiple_of(index * ROWS + j * TILE, TILE), TILE)
            own = pl.ds(pl.multiple_of(own_rows[0, at], TILE), TILE)
            total = totals[j % CHAINS]
            total[own, :] = total[own, :] + filt[rows, :].astype(jnp.float32) * h
        return carry

    lax.fori_loop(0, bodies_of(step, count), one, 0)

    @pl.when(step == pl.num_programs(0) - 1)
    def _():
        cast = sum(total[...] for total in totals).astype(jnp.bfloat16)
        pre = jnp.dot(cast, out_w[...], preferred_element_type=jnp.float32) + out_b[...]
        act = (softplus(pre) - LOG_TWO).astype(jnp.bfloat16)
        update = jnp.dot(act, fin_w[...], preferred_element_type=jnp.float32) + fin_b[...]
        new[...] = (feats[...].astype(jnp.float32) + update).astype(jnp.bfloat16)
        d_out = nt_dot(cot[...], fin_w[...])
        d_pre = (d_out * jax.nn.sigmoid(pre)).astype(jnp.bfloat16)
        grad[...] = nt_dot(d_pre, out_w[...])


def back_kernel(
    count, order, own_rows, other_rows, filt, filt_d, h0, h1, h2, h3, h4, g0, g1, g2, g3, g4, own_h, own_g,
    r_near, r_own, cot, in_w, grad, force, near, g_near, *totals
):
    step = pl.program_id(0)
    pushes = totals[CHAINS:]
    totals = totals[:CHAINS]

    @pl.when(step == 0)
    def _():
        laid_end_to_end((h0, h1, h2, h3, h4), near)
        laid_end_to_end((g0, g1, g2, g3, g4), g_near)
        for total in (*totals, *pushes):
            total[...] = jnp.zeros_like(total)

    def one(index, carry):
        slopes = []
        places = []
        for j in range(BODY):
            at = (step * STEP + index) * BODY + j
            slab = order[0, at]
            row = pl.ds(other_rows[0, at], 1)
            h = near[row, :]
            g = g_near[row, :]
            rows = pl.ds(pl.multiple_of(index * ROWS + j * TILE, TILE), TILE)
            own = pl.ds(pl.multiple_of(own_rows[0, at], TILE), TILE)
            total = totals[j % CHAINS]
            total[own, :] = total[own, :] + filt[rows, :].astype(jnp.float32) * g
            mixed = filt_d[rows, :].astype(jnp.float32) * (own_g[own, :] * h + own_h[own, :] * g)
            slopes.append(mixed.astype(jnp.bfloat16))
            places.append((own, slab))
        sums = jnp.dot(
            jnp.concatenate(slopes, axis=0),
            jnp.ones((128, 128), jnp.bfloat16),
            preferred_element_type=jnp.float32,
        )
        for j, (own, slab) in enumerate(places):
            push = pushes[j % CHAINS]
            push[own, :] = push[own, :] + sums[j * TILE : (j + 1) * TILE, :] * r_near[pl.ds(slab, 1), :]
        return carry

    lax.fori_loop(0, bodies_of(step, count), one, 0)

    @pl.when(step == pl.num_programs(0) - 1)
    def _():
        cast = sum(total[...] for total in totals).astype(jnp.bfloat16)
        grad[...] = cot[...].astype(jnp.float32) + nt_dot(cast, in_w[...])
        moments = sum(push[...] for push in pushes).T
        force[...] = moments[0:3, :] - r_own[...] * moments[3:4, :]


def pair_call(body, scalars, streams, arrays, outs, tables, scratch, name):
    stream = pl.BlockSpec((STEP * ROWS, 128), lambda s, n, *_: (last_block(s, n), 0))
    return pl.pallas_call(
        body,
        grid_spec=pltpu.PrefetchScalarGridSpec(
            num_scalar_prefetch=4,
            grid=(STEPS,),
            in_specs=[stream] * len(streams) + [whole(a) for a in arrays],
            out_specs=[whole(o) for o in outs],
            scratch_shapes=[pltpu.VMEM((AROUND_ROWS, 128), jnp.float32)] * tables
            + [pltpu.VMEM((256, 128), jnp.float32)] * scratch,
        ),
        out_shape=outs,
        compiler_params=pltpu.CompilerParams(vmem_limit_bytes=VMEM),
        name=name,
    )(*scalars, *streams, *arrays)


def swapped(to_far, to_near, axis):
    size = lax.axis_size(axis)
    near = [(i, i ^ 1) for i in range(size)]
    far = [(i, ((i ^ 1) + 2 * (2 * (i % 2) - 1)) % size) for i in range(size)]
    from_far = lax.ppermute(to_far, axis, far)
    return lax.ppermute(to_near, axis, near), from_far


def planes(own):
    near, far = swapped(own, own, "gz")
    return jnp.concatenate([near, own, far], axis=0)


def columns(three):
    near, far = swapped(three, three, "gx")
    return [near, three, far]


def on_device(
    features,
    positions,
    counts,
    pair_tiles,
    input_weight,
    radial_weight,
    radial_bias,
    filter_weight,
    filter_bias,
    output_weight,
    output_bias,
    final_weight,
    final_bias,
    cotangent,
):
    own_features = features.reshape(256, 128)
    own_pos = positions.reshape(3, 256)
    hidden = jnp.dot(own_features, input_weight, preferred_element_type=jnp.float32)
    numbers = jnp.concatenate([counts.reshape(1), pair_tiles.reshape(56)]).astype(jnp.float32)
    meta = jnp.concatenate(
        [own_pos.reshape(6, 128), jnp.pad(numbers, (0, 71))[None], jnp.zeros((1, 128), jnp.float32)],
        axis=0,
    )
    three = planes(jnp.concatenate([hidden, meta], axis=0)[None])
    meta_three = three[:, 256:].reshape(1, 24 * 128)
    hidden_three = three[:, :256].reshape(768, 128)

    across = lax.axis_size("gy")
    along = lax.axis_size("gx")
    everyone = lax.all_to_all(
        jnp.broadcast_to(meta_three.reshape(1, 24, 128), (along * across, 24, 128)),
        ("gx", "gy"),
        0,
        0,
    ).reshape(along * across, 24 * 128)
    everyone = everyone.reshape(along * across * 3, 8 * 128)
    side = np.array(SLOTS)
    sides = np.zeros((SLOT_ROWS, 4), np.int32)
    sides[:28, :3] = side
    sides[:28, 3] = 1
    selectors = [list_selectors((-1, 1)), list_selectors((1, -1))]
    where = jnp.stack([lax.axis_index(axis) for axis in ("gx", "gy", "gz")]).astype(jnp.int32)
    table, order, own_rows, other_rows, lists, count, at_unit = prepare(
        where,
        everyone,
        jnp.asarray(np.stack([rows for rows, _ in selectors])),
        jnp.asarray(np.stack([lanes for _, lanes in selectors])),
        jnp.asarray(list_bases()),
        jnp.asarray(sides),
        jnp.asarray(sides[:, :3].astype(np.float32)),
        own_pos.reshape(3, 8, TILE).transpose(0, 2, 1).reshape(96, 8),
    )
    near_x = columns(hidden_three)
    to_near, to_far, count = lax.optimization_barrier((*gather_tiles(lists, near_x), count))
    near = [*near_x, *swapped(to_far, to_near, "gy")]
    filt, filt_d = filters(
        count,
        order,
        table,
        radial_weight,
        filter_weight,
        radial_bias[None],
        filter_bias[None],
    )
    cot = cotangent.reshape(256, 128)
    scalars = (count, order, own_rows, other_rows)
    new_features, d_msg = pair_call(
        message_kernel,
        scalars,
        [filt],
        [
            *near,
            own_features,
            cot,
            output_weight,
            output_bias[None],
            final_weight,
            final_bias[None],
        ],
        [
            jax.ShapeDtypeStruct((256, 128), jnp.bfloat16),
            jax.ShapeDtypeStruct((256, 128), jnp.float32),
        ],
        1,
        CHAINS,
        "messages_and_update",
    )
    g_x = columns(planes(d_msg))
    to_near, to_far = gather_tiles(lists, g_x)
    g_near = [*g_x, *swapped(to_far, to_near, "gy")]
    r_near = at_unit.reshape(2 * SLOT_ROWS, 4, TILE).transpose(0, 2, 1).reshape(WIDE, 4)
    r_near = jnp.pad(r_near, ((0, 0), (0, 124)))
    grad_features, force = pair_call(
        back_kernel,
        scalars,
        [filt, filt_d],
        [*near, *g_near, hidden, d_msg, r_near, own_pos, cot, input_weight],
        [
            jax.ShapeDtypeStruct((256, 128), jnp.float32),
            jax.ShapeDtypeStruct((3, 256), jnp.float32),
        ],
        2,
        2 * CHAINS,
        "pair_gradients",
    )
    return (
        new_features.reshape(1, 1, 1, 256, 128),
        grad_features.reshape(1, 1, 1, 256, 128),
        force.reshape(1, 1, 1, 3, 256),
    )


def solution(mesh):
    block = P("gx", "gy", "gz", None, None)
    return jax.shard_map(
        on_device,
        mesh=mesh,
        in_specs=(
            block,
            block,
            P("gx", "gy", "gz"),
            P("gx", "gy", "gz", None, None, None),
            *([P()] * 9),
            block,
        ),
        out_specs=(block, block, block),
        check_vma=False,
    )
```

```python
import math

import jax
import jax.numpy as jnp
import numpy as np
from jax import lax
from jax.experimental import pallas as pl
from jax.experimental.pallas import tpu as pltpu
from jax.sharding import PartitionSpec as P

TILE = 32
SOFTEN = 0.05
GAMMA = 40.0
LOG_TWO = math.log(2.0)
KAPPA = math.sqrt(GAMMA / LOG_TWO)
UNITS = 56
VMEM = 56 * 1024 * 1024


def half_shell():
    offsets = [(0, 0, 0), (1, 0, 0)]
    for step_x in (-1, 0, 1):
        offsets.append((step_x, 1, 0))
    for step_x in (-1, 0, 1):
        for step_y in (-1, 0, 1):
            offsets.append((step_x, step_y, 1))
    return offsets


SHELL = half_shell()
AROUND = [
    (sx, sy, sz)
    for sy in (0, 1, -1)
    for sx in (-1, 0, 1)
    for sz in (-1, 0, 1)
    if (sx, sy, sz) != (0, 0, 0)
]
SLOTS = [(0, 0, 0), (0, 0, 0)] + AROUND


def shell_place(offset):
    if offset in SHELL:
        return SHELL.index(offset), True
    return SHELL.index(tuple(-step for step in offset)), False


SLOT_ROWS = 32
LIST_ROWS = 56
SENT = [(sx, sz) for sx in (-1, 0, 1) for sz in (-1, 0, 1)]


def list_selectors(sides):
    rows = {0: (SLOTS[0], SLOTS[0], 0, True), 1: (SLOTS[0], SLOTS[0], 0, False)}
    for i, offset in enumerate(AROUND):
        rows[2 + i] = (SLOTS[0], offset, *shell_place(offset))
    for j, side in enumerate(sides):
        for m, (sx, sz) in enumerate(SENT):
            offset = (sx, side, sz)
            rows[SLOT_ROWS + 9 * j + m] = ((0, -side, 0), offset, *shell_place(offset))
    holders = np.zeros((LIST_ROWS, SLOT_ROWS), np.float32)
    lanes = np.zeros((4, LIST_ROWS, 128), np.float32)
    for i, (reader, offset, index_k, ahead) in rows.items():
        holder = reader if ahead else tuple(a + b for a, b in zip(reader, offset))
        holders[i, SLOTS.index(holder)] = 1.0
        for q in range(4):
            lanes[q, i, 1 + 4 * index_k + (q if ahead else (q + 2) % 4)] = 1.0
    return holders, lanes


def list_bases():
    def place_of(steps, odd):
        return 1 - steps * (1 - 2 * odd)

    def rows(odd_x, odd_y, odd_z):
        bases = np.zeros((LIST_ROWS, 3), np.float32)
        for i, (sx, sy, sz) in enumerate(SLOTS):
            if sy == 0:
                first = (place_of(sx, odd_x) * 3 + place_of(sz, odd_z)) * 256
                bases[i] = first, first, TILE
            else:
                listed = (sx + 1) * 3 + sz + 1
                first = NINE + 576 * place_of(sy, odd_y) // 2 + listed * 2 * TILE
                bases[i] = first, first + TILE, 0
        for i, (sx, sz) in enumerate(SENT):
            first = (place_of(sx, odd_x) * 3 + place_of(sz, odd_z)) * 256
            for at in (SLOT_ROWS + i, SLOT_ROWS + 9 + i):
                bases[at] = first, first, TILE
        return bases

    even = rows(0, 0, 0)
    return np.stack([even, rows(1, 0, 0) - even, rows(0, 1, 0) - even, rows(0, 0, 1) - even])


def whole(array):
    return pl.BlockSpec(array.shape, lambda s, *_: (0,) * array.ndim)


def exact_dot(a, b):
    return jnp.dot(a, b, precision=lax.Precision.HIGHEST)


BODY = 64
ROWS = BODY * TILE
SLABS = UNITS * TILE
NINE = 9 * 256
AROUND_ROWS = NINE + 2 * 18 * TILE
BODIES = SLABS // BODY
WIDE = 2 * SLOT_ROWS * TILE
IDLE = 28 * TILE
STEP = 2
STEPS = BODIES // STEP


def prepare_kernel(
    where, everyone, holders, lanes, bases, side, shift, own_side,
    table, order, own_rows, other_rows, lists, count, at_unit
):
    f32 = jnp.float32
    odd = [where[a] & 1 for a in range(3)]
    device = ((where[0] + side[:, 0:1]) & 3) * 4 + ((where[1] + side[:, 1:2]) & 3)
    device = device * 3 + 1 - side[:, 2:3] * (1 - 2 * odd[2])
    device = jnp.where(side[:, 3:4] > 0, device, -1)
    devices = lax.broadcasted_iota(jnp.int32, (SLOT_ROWS, 48), 1)
    slots = exact_dot(jnp.where(devices == device, 1.0, 0.0), everyone[...])
    numbers = slots[:, 768:896]
    rows = exact_dot(holders[odd[1]], numbers)
    tiles = [jnp.sum(rows * lanes[odd[1], q], axis=1, keepdims=True) for q in range(4)]
    lane = lax.broadcasted_iota(jnp.int32, (LIST_ROWS, 128), 1)
    base = bases[0]
    for a in range(3):
        base = base + bases[1 + a] * odd[a].astype(f32)
    place = [base[:, n : n + 1] + base[:, 2:3] * tiles[2 + n] for n in range(2)]
    listed = jnp.where(lane < 1, tiles[0], jnp.where(lane < 2, tiles[1], place[1]))
    listed = jnp.where(lane == 2, place[0], listed)
    lists[...] = jnp.round(listed.T[0:8, :]).astype(jnp.int32)

    slot = lax.broadcasted_iota(jnp.int32, (SLOT_ROWS, 1), 0)
    halves = []
    for n in range(2):
        own = tiles[n][0:SLOT_ROWS]
        other = tiles[2 + n][0:SLOT_ROWS]
        at = []
        for c in range(3):
            acc = jnp.zeros((SLOT_ROWS, TILE), f32)
            for t in range(8):
                first = c * 256 + t * TILE
                acc = acc + jnp.where(jnp.abs(other - t) < 0.5, slots[:, first : first + TILE], 0.0)
            at.append(acc + shift[:, c : c + 1])
        same = jnp.where((jnp.abs(own - other) < 0.5) & (slot < 2), 1.0, 0.0)
        own_left = numbers[0:1, 0:1] - own * TILE
        other_left = numbers[:, 0:1] - other * TILE
        rest = jnp.where(lane[0:SLOT_ROWS, 0:TILE] == 0, own, 0.0)
        for q, value in enumerate((own_left, other_left, same, place[n][0:SLOT_ROWS] * (1.0 / TILE))):
            rest = jnp.where(lane[0:SLOT_ROWS, 0:TILE] == q + 1, value, rest)
        halves.append(jnp.concatenate([*at, rest], axis=1))
    per_unit = jnp.concatenate(halves, axis=0)
    one_beside = lax.broadcasted_iota(jnp.int32, (2 * SLOT_ROWS, 128), 1) >= 96
    at_unit[...] = jnp.where(one_beside, 1.0, per_unit)
    unit = lax.broadcasted_iota(jnp.int32, (2 * SLOT_ROWS, WIDE), 0)
    slab = lax.broadcasted_iota(jnp.int32, (2 * SLOT_ROWS, WIDE), 1)
    units = jnp.where(unit == (slab >> 5), 1.0, 0.0).astype(jnp.bfloat16)
    per_slab = jnp.dot(
        in_thirds(per_unit.T), jnp.concatenate([units] * 3, axis=0), preferred_element_type=f32
    )

    slab = lax.broadcasted_iota(jnp.int32, (TILE, WIDE), 1)
    u = lax.broadcasted_iota(jnp.int32, (TILE, WIDE), 0)
    w = slab & (TILE - 1)
    own_tile = per_slab[96:97]
    eight = lax.broadcasted_iota(jnp.int32, (8, WIDE), 0).astype(f32)
    chosen = jnp.where(jnp.abs(own_tile - eight) < 0.5, 1.0, 0.0).astype(jnp.bfloat16)
    own_at = jnp.dot(
        in_thirds(own_side[...]), jnp.concatenate([chosen] * 3, axis=0), preferred_element_type=f32
    )
    square = jnp.full((TILE, WIDE), SOFTEN * SOFTEN, f32)
    for c in range(3):
        part = slice(c * TILE, (c + 1) * TILE)
        other_at = jnp.sum(jnp.where(u == w, per_slab[part], 0.0), axis=0, keepdims=True)
        sep = other_at - own_at[part]
        square = square + sep * sep
    dist = jnp.sqrt(square)
    reverse = ((slab >> 5) & (SLOT_ROWS - 1)) == 1
    away = jnp.where(reverse, u - w, w - u)
    drop = (per_slab[99:100] > 0.5) & (away <= 0)
    fits = (u.astype(f32) < per_slab[97:98]) & (w.astype(f32) < per_slab[98:99])
    usable = fits & (dist < 1.0) & jnp.logical_not(drop)
    angle = math.pi * dist
    near = 1.0 / dist
    cut = jnp.where(usable, 0.5 * (jnp.cos(angle) + 1.0), 0.0)
    table[0:TILE, :] = KAPPA * dist
    table[TILE : 2 * TILE, :] = cut
    table[2 * TILE : 3 * TILE, :] = cut * (-2.0 * GAMMA / KAPPA) * near
    table[3 * TILE : 4 * TILE, :] = jnp.where(usable, -0.5 * math.pi * jnp.sin(angle), 0.0) * near

    live = jnp.max(jnp.where(usable, 1.0, 0.0), axis=0, keepdims=True)
    blocks = WIDE // 128
    live = jnp.concatenate([live[:, b * 128 : (b + 1) * 128] for b in range(blocks)], axis=0)
    row = lax.broadcasted_iota(jnp.int32, (128, 128), 0)
    col = lax.broadcasted_iota(jnp.int32, (128, 128), 1)
    upto = jnp.where(row <= col, 1.0, 0.0).astype(jnp.bfloat16)
    until = jnp.dot(live.astype(jnp.bfloat16), upto, preferred_element_type=f32)
    sums = jnp.broadcast_to(until[:, 127:128], (blocks, 128)).astype(jnp.bfloat16)
    below = jnp.where(row > col, 1.0, 0.0).astype(jnp.bfloat16)[0:blocks, 0:blocks]
    before = jnp.dot(below, sums, preferred_element_type=f32)
    rank = jnp.where(live > 0.5, until + before - 1.0, -1.0)
    total = before[blocks - 1 : blocks, :] + until[blocks - 1 : blocks, 127:128]
    bodies = jnp.floor((total + (BODY - 1.0)) * (1.0 / BODY))
    count[...] = jnp.broadcast_to(bodies, (8, 128)).astype(jnp.int32)
    target = lax.broadcasted_iota(jnp.int32, (256, 256), 0).astype(f32)
    names_row = lax.broadcasted_iota(jnp.int32, (8, 256), 0)
    names_lane = lax.broadcasted_iota(jnp.int32, (8, 256), 1)
    found = [jnp.zeros((8, 256), f32)] * (SLABS // 256)
    for b in range(blocks // 2):
        wide_rank = jnp.concatenate([rank[2 * b : 2 * b + 1], rank[2 * b + 1 : 2 * b + 2]], axis=1)
        names = jnp.where(names_row == 0, b * 8 + (names_lane >> 5), names_lane & (TILE - 1))
        names = jnp.where(names_row == 2, 1, names).astype(f32)
        part = slice(b * 256, (b + 1) * 256)
        names = jnp.where(names_row == 3, per_slab[96:97, part], names)
        names = jnp.where(names_row == 4, per_slab[100:101, part], names)
        names = names.astype(jnp.bfloat16)
        for i in range(min(b + 1, len(found))):
            hit = jnp.where(target == wide_rank - i * 256.0, 1.0, 0.0).astype(jnp.bfloat16)
            found[i] = found[i] + nt_dot(names, hit)
    found = jnp.concatenate(found, axis=1)
    named = jnp.where(found[2:3] > 0.5, found[0:1] * TILE + found[1:2], 1.0 * IDLE)
    order[...] = jnp.round(named).astype(jnp.int32)
    own_rows[...] = jnp.round(found[3:4] * TILE).astype(jnp.int32)
    other_rows[...] = jnp.round(found[4:5] * TILE + found[1:2]).astype(jnp.int32)


def in_thirds(values):
    high = values.astype(jnp.bfloat16)
    rest = values - high.astype(jnp.float32)
    middle = rest.astype(jnp.bfloat16)
    low = (rest - middle.astype(jnp.float32)).astype(jnp.bfloat16)
    return jnp.concatenate([high, middle, low], axis=1)


def prepare(where, *arrays):
    outs = [
        jax.ShapeDtypeStruct((128, WIDE), jnp.float32),
        *[jax.ShapeDtypeStruct((1, SLABS), jnp.int32)] * 3,
        jax.ShapeDtypeStruct((8, LIST_ROWS), jnp.int32),
        jax.ShapeDtypeStruct((8, 128), jnp.int32),
        jax.ShapeDtypeStruct((2 * SLOT_ROWS, 128), jnp.float32),
    ]
    return pl.pallas_call(
        prepare_kernel,
        grid_spec=pltpu.PrefetchScalarGridSpec(
            num_scalar_prefetch=1,
            grid=(1,),
            in_specs=[whole(a) for a in arrays],
            out_specs=[whole(o) for o in outs],
        ),
        out_shape=outs,
        compiler_params=pltpu.CompilerParams(vmem_limit_bytes=VMEM),
        name="distances_and_live_rows",
    )(where, *arrays)


def last_block(step, count):
    return jnp.minimum(step, jnp.maximum((count[0, 0] + STEP - 1) // STEP - 1, 0))


def bodies_of(step, count):
    return jnp.clip(count[0, 0] - step * STEP, 0, STEP)


def filter_kernel(
    count, order, table, centres, first_128, second_128, first_b, second_b, out, out_d, first_w, second_w
):
    step = pl.program_id(0)

    @pl.when(step == 0)
    def _():
        for wide_w, weight in ((first_w, first_128), (second_w, second_128)):
            wide_w[...] = jnp.zeros_like(wide_w)
            wide_w[0:128, 0:128] = weight[...]
            wide_w[128:256, 128:256] = weight[...]


    def one(index, carry):
        spread = [[], [], [], []]
        for j in range(BODY):
            slab = order[0, (step * STEP + index) * BODY + j]
            lanes = pl.ds(pl.multiple_of((slab >> 7) << 7, 128), 128)
            lane = jnp.full((TILE, 128), slab & 127, jnp.int32)
            for q in range(4):
                values = table[q * TILE : (q + 1) * TILE, lanes]
                spread[q].append(jnp.take_along_axis(values, lane, axis=1, mode="promise_in_bounds"))
        x = jnp.concatenate(spread[0], axis=0) - centres[...]
        e = jnp.exp2(-(x * x))
        both = jnp.concatenate([e.astype(jnp.bfloat16), (x * e).astype(jnp.bfloat16)], axis=1)
        first = jnp.dot(both, first_w[...], preferred_element_type=jnp.float32)
        z = 1.0 + jnp.exp(first[:, 0:128] + first_b[...])
        act = jnp.log(z) - LOG_TWO
        deriv = first[:, 128:256]
        deriv = deriv - deriv * pltpu.reciprocal(z, approx=True)
        both2 = jnp.concatenate([act.astype(jnp.bfloat16), deriv.astype(jnp.bfloat16)], axis=1)
        second = jnp.dot(both2, second_w[...], preferred_element_type=jnp.float32)
        base = second[:, 0:128] + second_b[...]
        at_row = pl.ds(pl.multiple_of(index * ROWS, ROWS), ROWS)
        out[at_row, :] = (base * jnp.concatenate(spread[1], axis=0)).astype(jnp.bfloat16)
        out_d[at_row, :] = (
            second[:, 128:256] * jnp.concatenate(spread[2], axis=0)
            + base * jnp.concatenate(spread[3], axis=0)
        ).astype(jnp.bfloat16)
        return carry

    lax.fori_loop(0, bodies_of(step, count), one, 0)


def filters(count, order, table, first_w, second_w, first_b, second_b):
    centres = np.array(KAPPA * np.arange(128) / 128.0, np.float32)[None]
    arrays = [table, jnp.asarray(centres), first_w, second_w, first_b, second_b]
    wide = pl.BlockSpec((STEP * ROWS, 128), lambda s, n, *_: (last_block(s, n), 0))
    return pl.pallas_call(
        filter_kernel,
        grid_spec=pltpu.PrefetchScalarGridSpec(
            num_scalar_prefetch=2,
            grid=(STEPS,),
            in_specs=[whole(a) for a in arrays],
            out_specs=[wide, wide],
            scratch_shapes=[pltpu.VMEM((256, 256), jnp.bfloat16)] * 2,
        ),
        out_shape=[jax.ShapeDtypeStruct((SLABS * TILE, 128), jnp.bfloat16)] * 2,
        compiler_params=pltpu.CompilerParams(vmem_limit_bytes=VMEM),
        name="pair_filters",
    )(count, order, *arrays)


def laid_end_to_end(pieces, held):
    row = 0
    for piece in pieces:
        held[row : row + piece.shape[0], :] = piece[...]
        row += piece.shape[0]


def gather_kernel(lists, one_side, middle, other_side, near, far, held):
    laid_end_to_end((one_side, middle, other_side), held)

    def one(index, carry):
        a = pl.multiple_of(lists[2 + (index & 1), SLOT_ROWS + (index >> 1)], TILE)
        b = pl.multiple_of(lists[2 + (index & 1), SLOT_ROWS + 9 + (index >> 1)], TILE)
        o = pl.multiple_of(index * TILE, TILE)
        near[pl.ds(o, TILE), :] = held[pl.ds(a, TILE), :]
        far[pl.ds(o, TILE), :] = held[pl.ds(b, TILE), :]
        return carry

    lax.fori_loop(0, 18, one, 0)


def gather_tiles(lists, pieces):
    shape = (18 * TILE, 128)
    outs = [jax.ShapeDtypeStruct(shape, jnp.float32)] * 2
    return pl.pallas_call(
        gather_kernel,
        grid_spec=pltpu.PrefetchScalarGridSpec(
            num_scalar_prefetch=1,
            grid=(1,),
            in_specs=[whole(p) for p in pieces],
            out_specs=[whole(o) for o in outs],
            scratch_shapes=[pltpu.VMEM((NINE, 128), jnp.float32)],
        ),
        out_shape=outs,
        compiler_params=pltpu.CompilerParams(vmem_limit_bytes=VMEM),
        name="tiles_to_send",
    )(lists, *pieces)


def softplus(values):
    return jnp.maximum(values, 0.0) + jnp.log(1.0 + jnp.exp(-jnp.abs(values)))


def nt_dot(a, b):
    return lax.dot_general(a, b, (((1,), (1,)), ((), ())), preferred_element_type=jnp.float32)


CHAINS = 8


def message_kernel(
    count, order, own_rows, other_rows, filt, p0, p1, p2, p3, p4, feats, cot, out_w, out_b, fin_w, fin_b,
    new, grad, near, *totals
):
    step = pl.program_id(0)

    @pl.when(step == 0)
    def _():
        laid_end_to_end((p0, p1, p2, p3, p4), near)
        for total in totals:
            total[...] = jnp.zeros_like(total)

    def one(index, carry):
        for j in range(BODY):
            at = (step * STEP + index) * BODY + j
            h = near[pl.ds(other_rows[0, at], 1), :]
            rows = pl.ds(pl.multiple_of(index * ROWS + j * TILE, TILE), TILE)
            own = pl.ds(pl.multiple_of(own_rows[0, at], TILE), TILE)
            total = totals[j % CHAINS]
            total[own, :] = total[own, :] + filt[rows, :].astype(jnp.float32) * h
        return carry

    lax.fori_loop(0, bodies_of(step, count), one, 0)

    @pl.when(step == pl.num_programs(0) - 1)
    def _():
        cast = sum(total[...] for total in totals).astype(jnp.bfloat16)
        pre = jnp.dot(cast, out_w[...], preferred_element_type=jnp.float32) + out_b[...]
        act = (softplus(pre) - LOG_TWO).astype(jnp.bfloat16)
        update = jnp.dot(act, fin_w[...], preferred_element_type=jnp.float32) + fin_b[...]
        new[...] = (feats[...].astype(jnp.float32) + update).astype(jnp.bfloat16)
        d_out = nt_dot(cot[...], fin_w[...])
        d_pre = (d_out * jax.nn.sigmoid(pre)).astype(jnp.bfloat16)
        grad[...] = nt_dot(d_pre, out_w[...])


def back_kernel(
    count, order, own_rows, other_rows, filt, filt_d, h0, h1, h2, h3, h4, g0, g1, g2, g3, g4, own_h, own_g,
    r_near, r_own, cot, in_w, grad, force, near, g_near, *totals
):
    step = pl.program_id(0)
    pushes = totals[CHAINS:]
    totals = totals[:CHAINS]

    @pl.when(step == 0)
    def _():
        laid_end_to_end((h0, h1, h2, h3, h4), near)
        laid_end_to_end((g0, g1, g2, g3, g4), g_near)
        for total in (*totals, *pushes):
            total[...] = jnp.zeros_like(total)

    def one(index, carry):
        slopes = []
        places = []
        for j in range(BODY):
            at = (step * STEP + index) * BODY + j
            slab = order[0, at]
            row = pl.ds(other_rows[0, at], 1)
            h = near[row, :]
            g = g_near[row, :]
            rows = pl.ds(pl.multiple_of(index * ROWS + j * TILE, TILE), TILE)
            own = pl.ds(pl.multiple_of(own_rows[0, at], TILE), TILE)
            total = totals[j % CHAINS]
            total[own, :] = total[own, :] + filt[rows, :].astype(jnp.float32) * g
            mixed = filt_d[rows, :].astype(jnp.float32) * (own_g[own, :] * h + own_h[own, :] * g)
            slopes.append(mixed.astype(jnp.bfloat16))
            places.append((own, slab))
        sums = jnp.dot(
            jnp.concatenate(slopes, axis=0),
            jnp.ones((128, 128), jnp.bfloat16),
            preferred_element_type=jnp.float32,
        )
        for j, (own, slab) in enumerate(places):
            push = pushes[j % CHAINS]
            push[own, :] = push[own, :] + sums[j * TILE : (j + 1) * TILE, :] * r_near[pl.ds(slab, 1), :]
        return carry

    lax.fori_loop(0, bodies_of(step, count), one, 0)

    @pl.when(step == pl.num_programs(0) - 1)
    def _():
        cast = sum(total[...] for total in totals).astype(jnp.bfloat16)
        grad[...] = cot[...].astype(jnp.float32) + nt_dot(cast, in_w[...])
        moments = sum(push[...] for push in pushes).T
        force[...] = moments[0:3, :] - r_own[...] * moments[3:4, :]


def pair_call(body, scalars, streams, arrays, outs, tables, scratch, name):
    stream = pl.BlockSpec((STEP * ROWS, 128), lambda s, n, *_: (last_block(s, n), 0))
    return pl.pallas_call(
        body,
        grid_spec=pltpu.PrefetchScalarGridSpec(
            num_scalar_prefetch=4,
            grid=(STEPS,),
            in_specs=[stream] * len(streams) + [whole(a) for a in arrays],
            out_specs=[whole(o) for o in outs],
            scratch_shapes=[pltpu.VMEM((AROUND_ROWS, 128), jnp.float32)] * tables
            + [pltpu.VMEM((256, 128), jnp.float32)] * scratch,
        ),
        out_shape=outs,
        compiler_params=pltpu.CompilerParams(vmem_limit_bytes=VMEM),
        name=name,
    )(*scalars, *streams, *arrays)


def swapped(to_far, to_near, axis):
    size = lax.axis_size(axis)
    near = [(i, i ^ 1) for i in range(size)]
    far = [(i, ((i ^ 1) + 2 * (2 * (i % 2) - 1)) % size) for i in range(size)]
    from_far = lax.ppermute(to_far, axis, far)
    return lax.ppermute(to_near, axis, near), from_far


def planes(own):
    near, far = swapped(own, own, "gz")
    return jnp.concatenate([near, own, far], axis=0)


def columns(three):
    near, far = swapped(three, three, "gx")
    return [near, three, far]


def on_device(
    features,
    positions,
    counts,
    pair_tiles,
    input_weight,
    radial_weight,
    radial_bias,
    filter_weight,
    filter_bias,
    output_weight,
    output_bias,
    final_weight,
    final_bias,
    cotangent,
):
    own_features = features.reshape(256, 128)
    own_pos = positions.reshape(3, 256)
    hidden = jnp.dot(own_features, input_weight, preferred_element_type=jnp.float32)
    numbers = jnp.concatenate([counts.reshape(1), pair_tiles.reshape(56)]).astype(jnp.float32)
    meta = jnp.concatenate(
        [own_pos.reshape(6, 128), jnp.pad(numbers, (0, 71))[None], jnp.zeros((1, 128), jnp.float32)],
        axis=0,
    )
    three = planes(jnp.concatenate([hidden, meta], axis=0)[None])
    meta_three = three[:, 256:].reshape(1, 24 * 128)
    hidden_three = three[:, :256].reshape(768, 128)

    across = lax.axis_size("gy")
    along = lax.axis_size("gx")
    everyone = lax.all_to_all(
        jnp.broadcast_to(meta_three.reshape(1, 24, 128), (along * across, 24, 128)),
        ("gx", "gy"),
        0,
        0,
    ).reshape(along * across, 24 * 128)
    everyone = everyone.reshape(along * across * 3, 8 * 128)
    side = np.array(SLOTS)
    sides = np.zeros((SLOT_ROWS, 4), np.int32)
    sides[:28, :3] = side
    sides[:28, 3] = 1
    selectors = [list_selectors((-1, 1)), list_selectors((1, -1))]
    where = jnp.stack([lax.axis_index(axis) for axis in ("gx", "gy", "gz")]).astype(jnp.int32)
    table, order, own_rows, other_rows, lists, count, at_unit = prepare(
        where,
        everyone,
        jnp.asarray(np.stack([rows for rows, _ in selectors])),
        jnp.asarray(np.stack([lanes for _, lanes in selectors])),
        jnp.asarray(list_bases()),
        jnp.asarray(sides),
        jnp.asarray(sides[:, :3].astype(np.float32)),
        own_pos.reshape(3, 8, TILE).transpose(0, 2, 1).reshape(96, 8),
    )
    near_x = columns(hidden_three)
    to_near, to_far, count = lax.optimization_barrier((*gather_tiles(lists, near_x), count))
    near = [*near_x, *swapped(to_far, to_near, "gy")]
    filt, filt_d = filters(
        count,
        order,
        table,
        radial_weight,
        filter_weight,
        radial_bias[None],
        filter_bias[None],
    )
    cot = cotangent.reshape(256, 128)
    scalars = (count, order, own_rows, other_rows)
    new_features, d_msg = pair_call(
        message_kernel,
        scalars,
        [filt],
        [
            *near,
            own_features,
            cot,
            output_weight,
            output_bias[None],
            final_weight,
            final_bias[None],
        ],
        [
            jax.ShapeDtypeStruct((256, 128), jnp.bfloat16),
            jax.ShapeDtypeStruct((256, 128), jnp.float32),
        ],
        1,
        CHAINS,
        "messages_and_update",
    )
    g_x = columns(planes(d_msg))
    to_near, to_far = gather_tiles(lists, g_x)
    g_near = [*g_x, *swapped(to_far, to_near, "gy")]
    r_near = at_unit.reshape(2 * SLOT_ROWS, 4, TILE).transpose(0, 2, 1).reshape(WIDE, 4)
    r_near = jnp.pad(r_near, ((0, 0), (0, 124)))
    grad_features, force = pair_call(
        back_kernel,
        scalars,
        [filt, filt_d],
        [*near, *g_near, hidden, d_msg, r_near, own_pos, cot, input_weight],
        [
            jax.ShapeDtypeStruct((256, 128), jnp.float32),
            jax.ShapeDtypeStruct((3, 256), jnp.float32),
        ],
        2,
        2 * CHAINS,
        "pair_gradients",
    )
    return (
        new_features.reshape(1, 1, 1, 256, 128),
        grad_features.reshape(1, 1, 1, 256, 128),
        force.reshape(1, 1, 1, 3, 256),
    )


def solution(mesh):
    block = P("gx", "gy", "gz", None, None)
    return jax.shard_map(
        on_device,
        mesh=mesh,
        in_specs=(
            block,
            block,
            P("gx", "gy", "gz"),
            P("gx", "gy", "gz", None, None, None),
            *([P()] * 9),
            block,
        ),
        out_specs=(block, block, block),
        check_vma=False,
    )
```
